32 devices in a mesh: ctx: 8 (over z, y), head: 4 (over x, core).
Axes of the slice: x: 2, y: 2, z: 4, core: 2. Of those that a mesh axis runs over, the one named last changes fastest.
Arguments:
- frozen_queries: bfloat16 [2048, 2048], P('ctx', 'head'), may hold values from -70 to 70
- key_value_rows: bfloat16 [2048, 512], P('ctx'), may hold values from -4.5 to 4.5
- output_gradient: bfloat16 [2048, 2048], P('ctx', 'head'), may hold values from -6 to 6
- inputs: bfloat16 [2048, 8192], P('ctx', 'head'), may hold values from -6 to 6
- adapter_down: float32 [64, 8192], P('ctx', 'head'), may hold values from -0.0625 to 0.0625
- down_first_moment: float32 [64, 8192], P('ctx', 'head'), may hold values from -6 to 6
- down_second_moment: float32 [64, 8192], P('ctx', 'head'), may hold values from 0.5 to 8
- adapter_up: float32 [64, 2048], P('ctx', 'head'), may hold values from -0.75 to 0.75
- up_first_moment: float32 [64, 2048], P('ctx', 'head'), may hold values from -6 to 6
- up_second_moment: float32 [64, 2048], P('ctx', 'head'), may hold values from 0.5 to 8
- rank_keep_mask: int32 [2, 64], replicated, may hold values 0 or 1
- group_length: int32 [2], replicated, may hold values from 256 to 1024, as said below
- group_shift: int32 [2], replicated, may hold values from 1 to 1023
Outputs:
- attention_out: bfloat16 [2048, 2048], P('ctx', 'head')
- query_gradient: bfloat16 [2048, 2048], P('ctx', 'head')
- kv_grad: float32 [2048, 512], P('ctx', 'head')
- updated_down: float32 [64, 8192], P('ctx', 'head')
- updated_down_first: float32 [64, 8192], P('ctx', 'head')
- updated_down_second: float32 [64, 8192], P('ctx', 'head')
- updated_up: float32 [64, 2048], P('ctx', 'head')
- updated_up_first: float32 [64, 2048], P('ctx', 'head')
- updated_up_second: float32 [64, 2048], P('ctx', 'head')
The draws below stay inside these ranges and needn't reach their ends.
Inputs may be any that keep to these rules, and one draw needn't show every extreme that they name: `group_length`: each key-value head's group holds 1024 rolled positions or fewer, and in every draw some head's group holds exactly 1024.
All inputs are finite; a program needn't handle non-finite values.
Results may differ from the reference program's by a relative error of at most 0.012.
Values may be sent and summed in bfloat16 or wider, within the bound.
A program may use at most 64 MiB of HBM per device.

```python
import math
import jax
import jax.numpy as jnp
from jax import lax

MODEL_WIDTH = 8192
LOCAL_HEADS = 16
KVH = 2
HEAD_SIZE = 128
ADAPTER_RANK = 64
TOK_DEV = 256
TOKENS = 2048
REACH = 4
GROUP = 1024
N_CTX = 8


def pair_table(key):
    shape_all = (TOKENS, 2 * KVH * HEAD_SIZE)
    table = jax.random.truncated_normal(jax.random.fold_in(key, 7003), -4.0, 4.0, shape_all, jnp.float32)
    return table


def draw_key_value_rows(key, part):
    return pair_table(key).astype(jnp.bfloat16)


def draw_frozen_queries(key, part):
    shape_all = (TOKENS, LOCAL_HEADS * HEAD_SIZE)
    base = jax.random.truncated_normal(jax.random.fold_in(key, 7005), -4.0, 4.0, shape_all, jnp.float32)
    return base.astype(jnp.bfloat16)


def draw_group_length(key, part):
    lengths = jax.random.randint(jax.random.fold_in(key, 7011), (KVH,), GROUP // 4, GROUP + 1)
    chosen = jax.random.randint(jax.random.fold_in(key, 7012), (), 0, KVH)
    return jnp.where(jnp.arange(KVH) == chosen, GROUP, lengths).astype(jnp.int32)


def with_ends(drawn, rng, least, top_value):
    spot = [jax.random.randint(jax.random.fold_in(rng, axis), (), 0, length) for axis, length in enumerate(drawn.shape)]
    main_axis = drawn.shape.index(max(drawn.shape))
    beside = spot[:main_axis] + [(spot[main_axis] + 1) % drawn.shape[main_axis]] + spot[main_axis + 1:]
    return drawn.at[tuple(spot)].set(least).at[tuple(beside)].set(top_value)


def block_levels(own_key, shape, split, smallest, largest):
    gain = 1.0
    for dim, blocks in split:
        steps = jax.random.uniform(jax.random.fold_in(jax.random.fold_in(own_key, 6), dim), (blocks,), jnp.float32, smallest / len(split), largest / len(split))
        gain = gain * jnp.repeat(jnp.exp(steps), shape[dim] // blocks).reshape((-1,) + (1,) * (len(shape) - 1 - dim))
    return gain


def normal_values(rng, dims, width, most, split=(), kind=jnp.bfloat16):
    factor_of = block_levels(rng, dims, split, -0.22, 0.18) if split else 1.0
    result = jax.random.normal(rng, dims, jnp.float32) * width * factor_of
    return jnp.minimum(jnp.maximum(result, -most), most).astype(kind)


def setup_inputs(seed: int = 0) -> dict:
    seeds = jax.random.split(jax.random.key(seed), 14)
    frozen_queries = draw_frozen_queries(jax.random.fold_in(seeds[13], 71), 0)
    key_value_rows = draw_key_value_rows(jax.random.fold_in(seeds[13], 71), 0)
    output_gradient = normal_values(seeds[2], (TOKENS, LOCAL_HEADS * HEAD_SIZE), 1.0, 6.0, ((0, 8), (1, 4)))
    inputs = normal_values(seeds[3], (TOKENS, MODEL_WIDTH), 1.0, 6.0, ((0, 8), (1, 4)))
    adapter_down = normal_values(seeds[4], (ADAPTER_RANK, MODEL_WIDTH), MODEL_WIDTH ** -0.5, 0.0625, ((0, 8), (1, 4)), jnp.float32)
    down_first_moment = normal_values(seeds[5], (ADAPTER_RANK, MODEL_WIDTH), 1.0, 6.0, ((0, 8), (1, 4)), jnp.float32)
    down_second_moment = jnp.clip(jnp.exp(math.log(8.0) - 2.7725887 * jax.random.uniform(seeds[6], (ADAPTER_RANK, MODEL_WIDTH), jnp.float32) ** block_levels(seeds[6], (ADAPTER_RANK, MODEL_WIDTH), ((0, 8), (1, 4)), -0.2, 0.2)), 0.5, 8.0)
    adapter_up = normal_values(seeds[7], (ADAPTER_RANK, LOCAL_HEADS * HEAD_SIZE), ADAPTER_RANK ** -0.5, 0.75, ((0, 8), (1, 4)), jnp.float32)
    up_first_moment = normal_values(seeds[8], (ADAPTER_RANK, LOCAL_HEADS * HEAD_SIZE), 1.0, 6.0, ((0, 8), (1, 4)), jnp.float32)
    up_second_moment = jnp.clip(jnp.exp(math.log(8.0) - 2.7725887 * jax.random.uniform(seeds[9], (ADAPTER_RANK, LOCAL_HEADS * HEAD_SIZE), jnp.float32) ** block_levels(seeds[9], (ADAPTER_RANK, LOCAL_HEADS * HEAD_SIZE), ((0, 8), (1, 4)), -0.2, 0.2)), 0.5, 8.0)
    rank_keep_mask = with_ends((jax.random.randint(seeds[10], (2, ADAPTER_RANK), 0, 2) < 1).astype(jnp.int32), jax.random.fold_in(seeds[10], 1), 0, 1)
    group_length = draw_group_length(jax.random.fold_in(seeds[13], 71), 0)
    group_shift = jax.random.randint(seeds[12], (KVH,), 1, GROUP).astype(jnp.int32)
    return dict(frozen_queries=frozen_queries, key_value_rows=key_value_rows, output_gradient=output_gradient, inputs=inputs, adapter_down=adapter_down, down_first_moment=down_first_moment, down_second_moment=down_second_moment, adapter_up=adapter_up, up_first_moment=up_first_moment, up_second_moment=up_second_moment, rank_keep_mask=rank_keep_mask, group_length=group_length, group_shift=group_shift)


adapter_scale = 0.25
beta_one = 0.9
beta_two = 0.999
learn_rate = 0.01
adam_epsilon = 1e-08

def adam_update(current, moment_one, moment_two, gradient):
    moment_one_new = beta_one * moment_one + (1.0 - beta_one) * gradient
    moment_two_new = beta_two * moment_two + (1.0 - beta_two) * gradient * gradient
    updated = current - learn_rate * moment_one_new / (jnp.sqrt(moment_two_new) + adam_epsilon)
    return (updated, moment_one_new, moment_two_new)

def reference(frozen_queries, key_value_rows, output_gradient, inputs, adapter_down, down_first_moment, down_second_moment, adapter_up, up_first_moment, up_second_moment, rank_keep_mask, group_length, group_shift):
    group_heads = LOCAL_HEADS // KVH
    seq_total = TOK_DEV * N_CTX
    span = (REACH + 1) * TOK_DEV
    down_keep_mask = rank_keep_mask[0].astype(jnp.float32)
    up_keep_mask = rank_keep_mask[1].astype(jnp.float32)
    half_down_factor = adapter_down.astype(jnp.bfloat16)
    masked_up_factor = adapter_up.astype(jnp.bfloat16) * rank_keep_mask[1][:, None].astype(jnp.bfloat16)
    projected = jnp.dot(inputs, half_down_factor.T, preferred_element_type=jnp.float32)
    masked_projection = (projected * down_keep_mask[None, :]).astype(jnp.bfloat16)
    query_values = (frozen_queries.astype(jnp.float32) + adapter_scale * jnp.dot(masked_projection, masked_up_factor, preferred_element_type=jnp.float32)).astype(jnp.bfloat16)
    score_scale = 1.0 / math.sqrt(HEAD_SIZE)
    query_blocks = query_values.reshape(N_CTX, TOK_DEV, KVH, group_heads, HEAD_SIZE)
    grad_blocks = output_gradient.reshape(N_CTX, TOK_DEV, KVH, group_heads, HEAD_SIZE)
    key_blocks = key_value_rows[:, :KVH * HEAD_SIZE].reshape(N_CTX, TOK_DEV, KVH, HEAD_SIZE)
    value_blocks = key_value_rows[:, KVH * HEAD_SIZE:].reshape(N_CTX, TOK_DEV, KVH, HEAD_SIZE)
    within = jnp.arange(TOK_DEV, dtype=jnp.int32)
    offsets = jnp.arange(REACH + 1, dtype=jnp.int32)

    def one_block(shard_index):
        sources = (shard_index - REACH + offsets + N_CTX) % N_CTX
        query_rows = query_blocks[shard_index].astype(jnp.float32)
        grad_rows = grad_blocks[shard_index].astype(jnp.float32)
        key_rows = key_blocks[sources].reshape(span, KVH, HEAD_SIZE).astype(jnp.float32)
        value_rows = value_blocks[sources].reshape(span, KVH, HEAD_SIZE).astype(jnp.float32)
        query_place = shard_index * TOK_DEV + within
        key_place = (sources[:, None] * TOK_DEV + within[None, :]).reshape(span)
        query_rolled = ((query_place[:, None] - group_shift[None, :]) % seq_total).T
        key_rolled = ((key_place[:, None] - group_shift[None, :]) % seq_total).T
        same_group = query_rolled[:, :, None] // group_length[:, None, None] == key_rolled[:, None, :] // group_length[:, None, None]
        allowed = same_group & (key_rolled[:, None, :] <= query_rolled[:, :, None])
        scores = jnp.einsum('qjhd,kjd->jhqk', query_rows, key_rows) * score_scale
        scores = jnp.where(allowed[:, None], scores, -1e+30)
        row_max = lax.optimization_barrier(jnp.max(scores, -1, keepdims=True))
        powers = jnp.exp(scores - row_max)
        weights = powers / lax.optimization_barrier(jnp.sum(powers, -1, keepdims=True))
        weights_half = lax.optimization_barrier(weights.astype(jnp.bfloat16)).astype(jnp.float32)
        attended = jnp.einsum('jhqk,kjd->qjhd', weights_half, value_rows).astype(jnp.bfloat16)
        grad_weights = jnp.einsum('qjhd,kjd->jhqk', grad_rows, value_rows)
        row_dots = lax.optimization_barrier(jnp.sum(weights * grad_weights, -1, keepdims=True))
        grad_scores = lax.optimization_barrier((weights * (grad_weights - row_dots)).astype(jnp.bfloat16)).astype(jnp.float32)
        grad_query = (score_scale * jnp.einsum('jhqk,kjd->qjhd', grad_scores, key_rows)).astype(jnp.bfloat16)
        grad_keys = score_scale * jnp.einsum('jhqk,qjhd->kjd', grad_scores, query_rows)
        grad_values = jnp.einsum('jhqk,qjhd->kjd', weights_half, grad_rows)
        return (attended, grad_query, grad_keys.reshape(REACH + 1, TOK_DEV, KVH, HEAD_SIZE), grad_values.reshape(REACH + 1, TOK_DEV, KVH, HEAD_SIZE))
    attended_all, grad_query_all, grad_keys_all, grad_values_all = lax.map(one_block, jnp.arange(N_CTX, dtype=jnp.int32))
    attention_out = attended_all.reshape(seq_total, LOCAL_HEADS * HEAD_SIZE)
    query_gradient = grad_query_all.reshape(seq_total, LOCAL_HEADS * HEAD_SIZE)
    key_total = grad_keys_all[:, REACH]
    value_total = grad_values_all[:, REACH]
    for back in range(REACH):
        key_total = key_total + jnp.roll(grad_keys_all[:, back], -(REACH - back), axis=0)
        value_total = value_total + jnp.roll(grad_values_all[:, back], -(REACH - back), axis=0)
    kv_grad = jnp.concatenate([key_total.reshape(seq_total, KVH * HEAD_SIZE), value_total.reshape(seq_total, KVH * HEAD_SIZE)], 1)
    up_gradient = up_keep_mask[:, None] * (adapter_scale * jnp.dot(masked_projection.T, query_gradient, preferred_element_type=jnp.float32))
    projection_backward = jnp.dot(query_gradient, masked_up_factor.T, preferred_element_type=jnp.float32)
    rank_product = (projection_backward * down_keep_mask[None, :] * adapter_scale).astype(jnp.bfloat16)
    down_gradient = jnp.dot(rank_product.T, inputs, preferred_element_type=jnp.float32)
    updated_down, updated_down_first, updated_down_second = adam_update(adapter_down, down_first_moment, down_second_moment, down_gradient)
    updated_up, updated_up_first, updated_up_second = adam_update(adapter_up, up_first_moment, up_second_moment, up_gradient)
    return (attention_out, query_gradient, kv_grad, updated_down, updated_down_first, updated_down_second, updated_up, updated_up_first, updated_up_second)
```

```python
import functools
import math

import jax
import jax.numpy as jnp
from jax import lax
from jax.experimental import pallas as pl
from jax.experimental.pallas import tpu as pltpu
from jax.sharding import PartitionSpec as P

LOCAL_HEADS = 16
KVH = 2
HEAD_SIZE = 128


adapter_scale = 0.25
beta_one = 0.9
beta_two = 0.999
learn_rate = 0.01
adam_epsilon = 1e-08


def shifted(value, axis, steps):
    count = lax.axis_size(axis)
    pairs = [(source, (source + steps) % count) for source in range(count)]
    return lax.ppermute(value, axis, pairs)


def adam_update(current, moment_one, moment_two, gradient):
    moment_one_new = beta_one * moment_one + (1.0 - beta_one) * gradient
    moment_two_new = beta_two * moment_two + (1.0 - beta_two) * gradient * gradient
    updated = current - learn_rate * moment_one_new / (jnp.sqrt(moment_two_new) + adam_epsilon)
    return (updated, moment_one_new, moment_two_new)


def spread_pair(key_part, value_part, head_slot, key_width):
    holder = jnp.zeros((key_part.shape[0], 2 * key_width), jnp.float32)
    holder = lax.dynamic_update_slice_in_dim(holder, key_part, head_slot * key_part.shape[1], 1)
    return lax.dynamic_update_slice_in_dim(
        holder, value_part, key_width + head_slot * key_part.shape[1], 1
    )


def on_device(
    frozen_queries,
    key_value_rows,
    output_gradient,
    inputs,
    adapter_down,
    down_first_moment,
    down_second_moment,
    adapter_up,
    up_first_moment,
    up_second_moment,
    rank_keep_mask,
    group_length,
    group_shift,
):
    tokens_here = frozen_queries.shape[0]
    ctx_count = lax.axis_size("ctx")
    ctx_place = lax.axis_index("ctx")
    head_place = lax.axis_index("head")
    reach = min(8, ctx_count // 2)
    heads_here = frozen_queries.shape[1] // HEAD_SIZE
    group_heads = LOCAL_HEADS // KVH
    kv_head = head_place * heads_here // group_heads
    seq_total = tokens_here * ctx_count
    key_width = KVH * HEAD_SIZE
    down_keep_mask = rank_keep_mask[0].astype(jnp.float32)
    down_full, up_full = (
        lax.all_gather(adapter_down.astype(jnp.bfloat16), "ctx", axis=0, tiled=True),
        lax.all_gather(adapter_up.astype(jnp.bfloat16), "ctx", axis=0, tiled=True),
    )
    masked_up_factor = up_full * rank_keep_mask[1][:, None].astype(jnp.bfloat16)
    contract_last = (((1,), (1,)), ((), ()))
    contract_first = (((0,), (0,)), ((), ()))
    projected = lax.psum(
        lax.dot_general(
            inputs, down_full, contract_last, preferred_element_type=jnp.float32
        ).astype(jnp.bfloat16),
        "head",
    ).astype(jnp.float32)
    masked_projection = (projected * down_keep_mask[None, :]).astype(jnp.bfloat16)
    query_values = (
        frozen_queries.astype(jnp.float32)
        + adapter_scale
        * jnp.dot(masked_projection, masked_up_factor, preferred_element_type=jnp.float32)
    ).astype(jnp.bfloat16)
    key_own = lax.dynamic_slice_in_dim(key_value_rows, kv_head * HEAD_SIZE, HEAD_SIZE, 1)
    value_own = lax.dynamic_slice_in_dim(
        key_value_rows, key_width + kv_head * HEAD_SIZE, HEAD_SIZE, 1
    )
    pair_own = jnp.concatenate([key_own, value_own], 1)
    within = jnp.arange(tokens_here, dtype=jnp.int32)
    query_place = ctx_place * tokens_here + within
    offset_here = group_shift[kv_head]
    group_here = group_length[kv_head]
    query_rolled = (query_place - offset_here) % seq_total
    query_group = query_rolled // group_here
    score_scale = 1.0 / math.sqrt(HEAD_SIZE)
    query_heads = query_values.reshape(tokens_here, heads_here, HEAD_SIZE)
    grad_heads = output_gradient.reshape(tokens_here, heads_here, HEAD_SIZE)

    def tile_scores(pair_rows, distance):
        source = (ctx_place - distance + ctx_count) % ctx_count
        key_rolled = (source * tokens_here + within - offset_here) % seq_total
        allowed = (query_group[:, None] == (key_rolled // group_here)[None, :]) & (
            key_rolled[None, :] <= query_rolled[:, None]
        )
        scores = (
            jnp.einsum(
                "qhd,kd->hqk",
                query_heads,
                pair_rows[:, :HEAD_SIZE],
                preferred_element_type=jnp.float32,
            )
            * score_scale
        )
        return jnp.where(allowed[None], scores, -1e30)

    def stats_step(carry, pair_rows, distance):
        running_max, running_total = carry
        scores = tile_scores(pair_rows, distance)
        new_max = jnp.maximum(running_max, jnp.max(scores, -1, keepdims=True))
        running_total = running_total * jnp.exp(running_max - new_max) + jnp.sum(
            jnp.exp(scores - new_max), -1, keepdims=True
        )
        return (new_max, running_total)

    start_max = jnp.full((heads_here, tokens_here, 1), -1e30, jnp.float32)
    start_total = jnp.zeros((heads_here, tokens_here, 1), jnp.float32)
    start_stack = jnp.zeros((reach + 1, tokens_here, 2 * HEAD_SIZE), jnp.bfloat16)

    def first_turn(distance, state):
        held, stack, stats = state
        stack = lax.dynamic_update_index_in_dim(stack, held, distance, 0)
        stats = stats_step(stats, held, distance)
        held = shifted(held, "ctx", 1)
        return (held, stack, stats)

    held, stack, stats = lax.fori_loop(
        0, reach, first_turn, (pair_own, start_stack, (start_max, start_total))
    )
    stack = lax.dynamic_update_index_in_dim(stack, held, reach, 0)
    row_max, total = stats_step(stats, held, reach)

    def weights_of(scores):
        return jnp.exp(scores - row_max) / total

    def out_step(carry, pair_rows, distance):
        out_sum, dot_sum = carry
        weights = weights_of(tile_scores(pair_rows, distance))
        weights_half = weights.astype(jnp.bfloat16)
        out_sum = out_sum + jnp.einsum(
            "hqk,kd->qhd",
            weights_half,
            pair_rows[:, HEAD_SIZE:],
            preferred_element_type=jnp.float32,
        )
        grad_weights = jnp.einsum(
            "qhd,kd->hqk", grad_heads, pair_rows[:, HEAD_SIZE:], preferred_element_type=jnp.float32
        )
        dot_sum = dot_sum + jnp.sum(weights * grad_weights, -1, keepdims=True)
        return (out_sum, dot_sum)

    start_out = (
        jnp.zeros((tokens_here, heads_here, HEAD_SIZE), jnp.float32),
        jnp.zeros((heads_here, tokens_here, 1), jnp.float32),
    )

    def second_kept(distance, inner):
        return out_step(inner, lax.dynamic_index_in_dim(stack, distance, 0, False), distance)

    out_sum, row_dots = lax.fori_loop(0, reach + 1, second_kept, start_out)
    attention_out = out_sum.astype(jnp.bfloat16).reshape(tokens_here, heads_here * HEAD_SIZE)

    def grad_tile(pair_rows, distance):
        weights = weights_of(tile_scores(pair_rows, distance))
        weights_half = weights.astype(jnp.bfloat16)
        grad_weights = jnp.einsum(
            "qhd,kd->hqk", grad_heads, pair_rows[:, HEAD_SIZE:], preferred_element_type=jnp.float32
        )
        grad_scores = (weights * (grad_weights - row_dots)).astype(jnp.bfloat16)
        query_part = jnp.einsum(
            "hqk,kd->qhd", grad_scores, pair_rows[:, :HEAD_SIZE], preferred_element_type=jnp.float32
        )
        key_part = score_scale * jnp.einsum(
            "hqk,qhd->kd", grad_scores, query_heads, preferred_element_type=jnp.float32
        )
        value_part = jnp.einsum(
            "hqk,qhd->kd", weights_half, grad_heads, preferred_element_type=jnp.float32
        )
        return (query_part, jnp.concatenate([key_part, value_part], 1))

    start_query = jnp.zeros((tokens_here, heads_here, HEAD_SIZE), jnp.float32)
    start_pair = jnp.zeros((tokens_here, 2 * HEAD_SIZE), jnp.float32)

    def third_kept(index, state):
        grads_held, query_sum = state
        distance = reach - index
        query_part, pair_part = grad_tile(
            lax.dynamic_index_in_dim(stack, distance, 0, False), distance
        )
        grads_held = shifted((grads_held + pair_part).astype(jnp.bfloat16), "ctx", -1).astype(
            jnp.float32
        )
        return (grads_held, query_sum + query_part)

    grads_held, query_sum = lax.fori_loop(0, reach, third_kept, (start_pair, start_query))
    query_part, pair_part = grad_tile(pair_own, 0)
    query_sum = query_sum + query_part
    pair_total = grads_held + pair_part
    query_gradient = (
        (score_scale * query_sum).astype(jnp.bfloat16).reshape(tokens_here, heads_here * HEAD_SIZE)
    )
    holder = spread_pair(pair_total[:, :HEAD_SIZE], pair_total[:, HEAD_SIZE:], kv_head, key_width)
    kv_grad = lax.psum_scatter(
        holder.astype(jnp.bfloat16), "head", scatter_dimension=1, tiled=True
    ).astype(jnp.float32)
    projection_backward = lax.psum(
        lax.dot_general(
            query_gradient, masked_up_factor, contract_last, preferred_element_type=jnp.float32
        ).astype(jnp.bfloat16),
        "head",
    ).astype(jnp.float32)
    rank_product = (projection_backward * down_keep_mask[None, :] * adapter_scale).astype(
        jnp.bfloat16
    )
    part_down = lax.dot_general(
        rank_product, inputs, contract_first, preferred_element_type=jnp.float32
    )
    partial_up = adapter_scale * lax.dot_general(
        masked_projection, query_gradient, contract_first, preferred_element_type=jnp.float32
    )
    local_rows = adapter_down.shape[0]
    sum_down, sum_up = lax.psum((part_down, partial_up), "ctx")
    down_gradient = lax.dynamic_slice_in_dim(sum_down, ctx_place * local_rows, local_rows, 0)
    up_gradient = lax.dynamic_slice_in_dim(sum_up, ctx_place * local_rows, local_rows, 0)
    keep_rows = lax.dynamic_slice_in_dim(
        rank_keep_mask[1], ctx_place * local_rows, local_rows, 0
    ).astype(jnp.float32)
    up_gradient = keep_rows[:, None] * up_gradient
    updated_down, updated_down_first, updated_down_second = adam_update(
        adapter_down, down_first_moment, down_second_moment, down_gradient
    )
    updated_up, updated_up_first, updated_up_second = adam_update(
        adapter_up, up_first_moment, up_second_moment, up_gradient
    )
    return (
        attention_out,
        query_gradient,
        kv_grad,
        updated_down,
        updated_down_first,
        updated_down_second,
        updated_up,
        updated_up_first,
        updated_up_second,
    )


CONTRACT_LAST = (((1,), (1,)), ((), ()))
CONTRACT_FIRST = (((0,), (0,)), ((), ()))


def matmul(left, right, dims=(((1,), (0,)), ((), ()))):
    return lax.dot_general(left, right, dims, preferred_element_type=jnp.float32)


def remote(source, target, send_sem, recv_sem, device):
    return pltpu.make_async_remote_copy(
        src_ref=source,
        dst_ref=target,
        send_sem=send_sem,
        recv_sem=recv_sem,
        device_id=device,
        device_id_type=pl.DeviceIdType.MESH,
    )


def fused_kernel(
    ctx_count,
    frozen_ref,
    rows_ref,
    cotangent_ref,
    inputs_ref,
    down_ref,
    down_one_ref,
    down_two_ref,
    up_ref,
    up_one_ref,
    up_two_ref,
    mask_ref,
    length_ref,
    shift_ref,
    out_ref,
    query_grad_ref,
    kv_grad_ref,
    new_down_ref,
    new_down_one_ref,
    new_down_two_ref,
    new_up_ref,
    new_up_one_ref,
    new_up_two_ref,
    factors,
    down_full,
    up_full,
    pairs,
    proj_parts,
    rank_parts,
    weight_rows,
    score_rows,
    query_columns,
    grad_columns,
    own_part,
    core_send,
    core_parts,
    owner_send,
    owner_parts,
    sum_send,
    sum_parts,
    send_sems,
    factor_sems,
    pair_sems,
    proj_sems,
    rank_sems,
    core_sems,
    owner_sems,
    sum_sems,
):
    tokens = frozen_ref.shape[0]
    half = tokens // 2
    heads = frozen_ref.shape[1] // HEAD_SIZE
    reach = pairs.shape[0] - 1
    head_count = proj_parts.shape[0]
    local_rows = down_ref.shape[0]
    down_half = down_ref.shape[1] // 2
    up_half = up_ref.shape[1] // 2
    seq_total = tokens * ctx_count
    key_width = KVH * HEAD_SIZE
    score_scale = 1.0 / math.sqrt(HEAD_SIZE)
    place = lax.axis_index("ctx")
    lane = lax.axis_index("head")
    chip = lane // 2
    core = lane % 2
    odd = place % 2
    beside = place + 1 - 2 * odd
    other_core = lane + 1 - 2 * core
    final_lane = core * 2 + chip
    crossing = chip != core
    used = [0]
    sent = []

    def next_sem():
        used[0] += 1
        return send_sems.at[used[0] - 1]

    def away(steps):
        return lax.rem(place + steps + ctx_count, ctx_count)

    def send(source, target, recv_sem, device, when=None):
        copy = remote(source, target, next_sem(), recv_sem, device)
        if when is None:
            copy.start()
        else:
            pl.when(when)(copy.start)
        sent.append((copy, when))

    def arrived(target, recv_sem):
        remote(target, target, send_sems.at[0], recv_sem, (place, lane)).wait_recv()

    barrier = pltpu.get_barrier_semaphore()

    def greet(device):
        pl.semaphore_signal(
            barrier, inc=1, device_id=device, device_id_type=pl.DeviceIdType.MESH
        )

    for steps in range(1, ctx_count):
        greet((away(steps), lane))
    for steps in range(1, head_count):
        greet((place, lax.rem(lane + steps, head_count)))

    @pl.when(crossing)
    def _():
        for steps in range(1, ctx_count):
            greet((away(steps), final_lane))

    own_down = down_ref[...]
    own_up = up_ref[...]
    factors[place] = jnp.concatenate(
        [
            jnp.concatenate([own_down[:, :down_half], own_down[:, down_half:]], 0),
            jnp.concatenate([own_up[:, :up_half], own_up[:, up_half:]], 0),
        ],
        1,
    ).astype(jnp.bfloat16)
    key_start = pl.multiple_of(chip * HEAD_SIZE, HEAD_SIZE)
    pairs[0, :, :HEAD_SIZE] = rows_ref[:, pl.ds(key_start, HEAD_SIZE)]
    pairs[0, :, HEAD_SIZE:] = rows_ref[:, pl.ds(key_width + key_start, HEAD_SIZE)]

    straight_peers = ctx_count + head_count - 2

    @pl.when(crossing)
    def _():
        pl.semaphore_wait(barrier, straight_peers + ctx_count - 1)

    @pl.when(jnp.logical_not(crossing))
    def _():
        pl.semaphore_wait(barrier, straight_peers)

    def send_factors(owner, device_place):
        send(
            factors.at[owner], factors.at[owner], factor_sems.at[owner], (device_place, lane)
        )

    half_start = pl.multiple_of(core * half, half)

    def pair_half(slot, start):
        return pairs.at[slot, pl.ds(start, half)]

    def send_pair(slot, new_slot, device, when=None):
        send(
            pair_half(slot, half_start),
            pair_half(new_slot, half_start),
            pair_sems.at[new_slot, core],
            device,
            when,
        )

    for steps in range(2, ctx_count, 2):
        send_factors(place, away(steps))
    send_factors(place, beside)
    send_pair(0, 2, (away(2), lane))
    send_pair(0, 4, (away(4), lane))
    send_pair(0, 1, (beside, lane), odd == 0)
    for steps in range(2, ctx_count, 2):
        owner = away(steps)
        arrived(factors.at[owner], factor_sems.at[owner])
        send_factors(owner, beside)

    core_device = (place, other_core)
    arrived(pair_half(2, half_start), pair_sems.at[2, core])
    send_pair(2, 3, (beside, lane), odd == 0)
    send_pair(2, 1, (beside, lane), odd == 1)
    send_pair(2, 2, core_device)
    arrived(pair_half(4, half_start), pair_sems.at[4, core])
    send_pair(4, 3, (beside, lane), odd == 1)
    send_pair(4, 4, core_device)

    for steps in range(0, ctx_count, 2):
        owner = lax.rem(beside + steps, ctx_count)
        arrived(factors.at[owner], factor_sems.at[owner])

    mask_rows = mask_ref[...].astype(jnp.float32)
    rank_all = mask_rows.shape[1]
    diagonal = lax.broadcasted_iota(jnp.int32, (rank_all, rank_all), 0) == (
        lax.broadcasted_iota(jnp.int32, (rank_all, rank_all), 1)
    )

    def column(row):
        return jnp.sum(jnp.where(diagonal, row, 0.0), 1, keepdims=True)

    down_keep = column(mask_rows[0:1])
    up_keep = column(mask_rows[1:2])
    for owner in range(ctx_count):
        block = factors[owner].astype(jnp.float32)
        rows = slice(owner * local_rows, (owner + 1) * local_rows)
        down_full[rows, :down_half] = block[:local_rows, :down_half]
        down_full[rows, down_half:] = block[local_rows:, :down_half]
        up_full[rows, :up_half] = block[:local_rows, down_half:]
        up_full[rows, up_half:] = block[local_rows:, down_half:]
    masked_up = (up_full[...] * up_keep).astype(jnp.bfloat16)
    proj_parts[lane] = matmul(
        down_full[...].astype(jnp.bfloat16), inputs_ref[...], CONTRACT_LAST
    ).astype(jnp.bfloat16)

    def send_to_heads(parts, sems):
        for steps in range(1, head_count):
            send(
                parts.at[lane],
                parts.at[lane],
                sems.at[lane],
                (place, lax.rem(lane + steps, head_count)),
            )

    def sum_of_heads(parts, sems):
        for steps in range(1, head_count):
            source = lax.rem(lane + steps, head_count)
            arrived(parts.at[source], sems.at[source])
        total = parts[0].astype(jnp.float32)
        for source in range(1, head_count):
            total = total + parts[source].astype(jnp.float32)
        return total

    send_to_heads(proj_parts, proj_sems)
    for slot in (1, 3):
        arrived(pair_half(slot, half_start), pair_sems.at[slot, core])
        send_pair(slot, slot, core_device)
    other_start = pl.multiple_of((1 - core) * half, half)
    for slot in range(1, reach + 1):
        arrived(pair_half(slot, other_start), pair_sems.at[slot, 1 - core])
    for head in range(heads):
        grad_columns[:, head * tokens : (head + 1) * tokens] = (
            cotangent_ref[:, head * HEAD_SIZE : (head + 1) * HEAD_SIZE].astype(jnp.float32).T
        ).astype(jnp.bfloat16)

    length = length_ref[chip]
    first_rolled = lax.rem(place * tokens - shift_ref[chip] + seq_total, seq_total)
    first_inside = lax.rem(first_rolled, length)
    query_index = lax.broadcasted_iota(jnp.int32, (tokens, 1), 0)
    inside = first_inside + query_index
    inside = jnp.where(inside >= length, inside - length, inside)
    rolled = first_rolled + query_index
    inside = jnp.where(rolled >= seq_total, rolled - seq_total, inside)
    gap = lax.broadcasted_iota(jnp.int32, (tokens, tokens), 0) - lax.broadcasted_iota(
        jnp.int32, (tokens, tokens), 1
    )
    lower = gap >= 0
    allowed = [jnp.where(lower, gap, gap + reach * tokens) <= inside]
    for slot in range(1, reach):
        allowed.append(gap + slot * tokens <= inside)

    masked_proj = (sum_of_heads(proj_parts, proj_sems) * (down_keep * up_keep)).astype(
        jnp.bfloat16
    )
    span = (reach + 1) * tokens
    all_keys = pairs[:, :, :HEAD_SIZE].reshape(span, HEAD_SIZE)
    all_values = pairs[:, :, HEAD_SIZE:].reshape(span, HEAD_SIZE)

    def tiles_of(product):
        first = jnp.where(lower, product[:, :tokens], product[:, reach * tokens :])
        return [first] + [
            product[:, slot * tokens : (slot + 1) * tokens] for slot in range(1, reach)
        ]

    def spread(tiles):
        nothing = jnp.zeros_like(tiles[0])
        return jnp.concatenate(
            [jnp.where(lower, tiles[0], nothing)]
            + tiles[1:]
            + [jnp.where(lower, nothing, tiles[0])],
            1,
        ).astype(jnp.bfloat16)

    for head in range(heads):
        columns = slice(head * HEAD_SIZE, (head + 1) * HEAD_SIZE)
        rows = slice(head * tokens, (head + 1) * tokens)
        query = (
            frozen_ref[:, columns].astype(jnp.float32)
            + adapter_scale * matmul(masked_proj, masked_up[:, columns], CONTRACT_FIRST)
        )
        query_columns[:, rows] = query.astype(jnp.bfloat16).astype(jnp.float32).T.astype(
            jnp.bfloat16
        )
        query = query.astype(jnp.bfloat16)
        scores = [
            jnp.where(keep, tile * score_scale, -1e30)
            for keep, tile in zip(allowed, tiles_of(matmul(query, all_keys, CONTRACT_LAST)))
        ]
        row_max = jnp.max(
            jnp.maximum(jnp.maximum(scores[0], scores[1]), jnp.maximum(scores[2], scores[3])),
            1,
            keepdims=True,
        )
        powers = [jnp.exp(tile - row_max) for tile in scores]
        total = jnp.sum(powers[0] + powers[1] + powers[2] + powers[3], 1, keepdims=True)
        inverse = 1.0 / total
        weights = [tile * inverse for tile in powers]
        grad_weights = tiles_of(matmul(cotangent_ref[:, columns], all_values, CONTRACT_LAST))
        products = [tile * grad for tile, grad in zip(weights, grad_weights)]
        row_dots = jnp.sum(
            products[0] + products[1] + products[2] + products[3], 1, keepdims=True
        )
        grad_scores = spread(
            [tile * (grad - row_dots) for tile, grad in zip(weights, grad_weights)]
        )
        weights_half = spread(weights)
        weight_rows[rows, :] = weights_half
        score_rows[rows, :] = grad_scores
        out_ref[:, columns] = matmul(weights_half, all_values).astype(jnp.bfloat16)
        query_grad_ref[:, columns] = (score_scale * matmul(grad_scores, all_keys)).astype(
            jnp.bfloat16
        )

    query_grad = query_grad_ref[...]
    rank_parts[lane] = matmul(masked_up, query_grad, CONTRACT_LAST).astype(jnp.bfloat16)
    send_to_heads(rank_parts, rank_sems)

    for slot in range(reach, -1, -1):
        keys = slice(slot * tokens, (slot + 1) * tokens)
        key_part = score_scale * matmul(query_columns[...], score_rows[:, keys])
        value_part = matmul(grad_columns[...], weight_rows[:, keys])
        core_send[slot] = jnp.where(core == 0, value_part, key_part).astype(jnp.bfloat16)
        own_part[slot] = jnp.where(core == 0, key_part, value_part)
        send(core_send.at[slot], core_parts.at[slot], core_sems.at[slot], core_device)

    up_sum = adapter_scale * matmul(masked_proj, query_grad)

    for slot in range(reach, -1, -1):
        arrived(core_parts.at[slot], core_sems.at[slot])
        owner_send[slot] = (own_part[slot] + core_parts[slot].astype(jnp.float32)).astype(
            jnp.bfloat16
        )
        send(
            owner_send.at[slot],
            owner_parts.at[slot],
            owner_sems.at[slot],
            (away(-slot), final_lane),
            crossing if slot == 0 else None,
        )

    rank_product = (
        sum_of_heads(rank_parts, rank_sems) * (down_keep * adapter_scale)
    ).astype(jnp.bfloat16)
    down_sum = matmul(rank_product, inputs_ref[...])
    for owner in range(ctx_count):
        rows = slice(owner * local_rows, (owner + 1) * local_rows)
        sum_send[owner] = jnp.concatenate(
            [
                jnp.concatenate([down_sum[rows, :down_half], down_sum[rows, down_half:]], 0),
                jnp.concatenate([up_sum[rows, :up_half], up_sum[rows, up_half:]], 0),
            ],
            1,
        ).astype(jnp.bfloat16)
    for steps in range(1, ctx_count):
        owner = away(steps)
        send(
            sum_send.at[owner], sum_parts.at[place], sum_sems.at[place], (owner, lane)
        )
    gradient = sum_send[place].astype(jnp.float32)
    for steps in range(1, ctx_count):
        source = away(-steps)
        arrived(sum_parts.at[source], sum_sems.at[source])
        gradient = gradient + sum_parts[source].astype(jnp.float32)
    down_gradient = jnp.concatenate(
        [gradient[:local_rows, :down_half], gradient[local_rows:, :down_half]], 1
    )
    up_gradient = jnp.concatenate(
        [gradient[:local_rows, down_half:], gradient[local_rows:, down_half:]], 1
    )
    new_down_ref[...], new_down_one_ref[...], new_down_two_ref[...] = adam_update(
        own_down, down_one_ref[...], down_two_ref[...], down_gradient
    )
    new_up_ref[...], new_up_one_ref[...], new_up_two_ref[...] = adam_update(
        own_up, up_one_ref[...], up_two_ref[...], up_gradient
    )

    @pl.when(crossing)
    def _():
        arrived(owner_parts.at[0], owner_sems.at[0])

    @pl.when(jnp.logical_not(crossing))
    def _():
        owner_parts[0] = owner_send[0]

    part_sum = owner_parts[0].astype(jnp.float32)
    for slot in range(1, reach + 1):
        arrived(owner_parts.at[slot], owner_sems.at[slot])
        part_sum = part_sum + owner_parts[slot].astype(jnp.float32)
    kv_grad_ref[...] = part_sum.T

    for copy, when in sent:
        if when is None:
            copy.wait_send()
        else:
            pl.when(when)(copy.wait_send)


def fused(*args):
    frozen, rows, _, inputs, down, _, _, up = args[:8]
    ctx_count = lax.axis_size("ctx")
    head_count = lax.axis_size("head")
    reach = min(8, ctx_count // 2)
    tokens = frozen.shape[0]
    heads = frozen.shape[1] // HEAD_SIZE
    local_rows = down.shape[0]
    rank_all = local_rows * ctx_count
    block = (2 * local_rows, (down.shape[1] + up.shape[1]) // 2)
    half_type, full_type = jnp.bfloat16, jnp.float32
    in_vmem = pl.BlockSpec(memory_space=pltpu.VMEM)
    in_smem = pl.BlockSpec(memory_space=pltpu.SMEM)
    shapes = [
        (frozen.shape, half_type),
        (frozen.shape, half_type),
        ((tokens, HEAD_SIZE), full_type),
        (down.shape, full_type),
        (down.shape, full_type),
        (down.shape, full_type),
        (up.shape, full_type),
        (up.shape, full_type),
        (up.shape, full_type),
    ]
    return pl.pallas_call(
        functools.partial(fused_kernel, ctx_count),
        out_shape=[jax.ShapeDtypeStruct(shape, kind) for shape, kind in shapes],
        in_specs=[in_vmem] * 11 + [in_smem] * 2,
        out_specs=[in_vmem] * 9,
        scratch_shapes=[
            pltpu.VMEM((ctx_count,) + block, half_type),
            pltpu.VMEM((rank_all, down.shape[1]), full_type),
            pltpu.VMEM((rank_all, up.shape[1]), full_type),
            pltpu.VMEM((reach + 1, tokens, 2 * HEAD_SIZE), half_type),
            pltpu.VMEM((head_count, rank_all, tokens), half_type),
            pltpu.VMEM((head_count, rank_all, tokens), half_type),
            pltpu.VMEM((heads * tokens, (reach + 1) * tokens), half_type),
            pltpu.VMEM((heads * tokens, (reach + 1) * tokens), half_type),
            pltpu.VMEM((HEAD_SIZE, heads * tokens), half_type),
            pltpu.VMEM((HEAD_SIZE, heads * tokens), half_type),
            pltpu.VMEM((reach + 1, HEAD_SIZE, tokens), full_type),
            pltpu.VMEM((reach + 1, HEAD_SIZE, tokens), half_type),
            pltpu.VMEM((reach + 1, HEAD_SIZE, tokens), half_type),
            pltpu.VMEM((reach + 1, HEAD_SIZE, tokens), half_type),
            pltpu.VMEM((reach + 1, HEAD_SIZE, tokens), half_type),
            pltpu.VMEM((ctx_count,) + block, half_type),
            pltpu.VMEM((ctx_count,) + block, half_type),
            pltpu.SemaphoreType.DMA((64,)),
            pltpu.SemaphoreType.DMA((ctx_count,)),
            pltpu.SemaphoreType.DMA((reach + 1, 2)),
            pltpu.SemaphoreType.DMA((head_count,)),
            pltpu.SemaphoreType.DMA((head_count,)),
            pltpu.SemaphoreType.DMA((reach + 1,)),
            pltpu.SemaphoreType.DMA((reach + 1,)),
            pltpu.SemaphoreType.DMA((ctx_count,)),
        ],
        compiler_params=pltpu.CompilerParams(
            collective_id=0, has_side_effects=True, vmem_limit_bytes=40 * 1024 * 1024
        ),
    )(*args)


def on_any_mesh(*args):
    fits = (
        min(8, lax.axis_size("ctx") // 2) == 4
        and lax.axis_size("ctx") % 2 == 0
        and args[4].shape[0] % 8 == 0
        and lax.axis_size("head") == 2 * KVH
    )
    return tuple(fused(*args)) if fits else on_device(*args)


def solution(mesh):
    placed = (
        P("ctx", "head"),
        P("ctx", None),
        P("ctx", "head"),
        P("ctx", "head"),
        P("ctx", "head"),
        P("ctx", "head"),
        P("ctx", "head"),
        P("ctx", "head"),
        P("ctx", "head"),
        P("ctx", "head"),
        P(),
        P(),
        P(),
    )
    return jax.shard_map(
        on_any_mesh,
        mesh=mesh,
        in_specs=placed,
        out_specs=(
            P("ctx", "head"),
            P("ctx", "head"),
            P("ctx", "head"),
            P("ctx", "head"),
            P("ctx", "head"),
            P("ctx", "head"),
            P("ctx", "head"),
            P("ctx", "head"),
            P("ctx", "head"),
        ),
        check_vma=False,
    )
```

```python
import functools
import math

import jax
import jax.numpy as jnp
from jax import lax
from jax.experimental import pallas as pl
from jax.experimental.pallas import tpu as pltpu
from jax.sharding import PartitionSpec as P

LOCAL_HEADS = 16
KVH = 2
HEAD_SIZE = 128


adapter_scale = 0.25
beta_one = 0.9
beta_two = 0.999
learn_rate = 0.01
adam_epsilon = 1e-08


def shifted(value, axis, steps):
    count = lax.axis_size(axis)
    pairs = [(source, (source + steps) % count) for source in range(count)]
    return lax.ppermute(value, axis, pairs)


def adam_update(current, moment_one, moment_two, gradient):
    moment_one_new = beta_one * moment_one + (1.0 - beta_one) * gradient
    moment_two_new = beta_two * moment_two + (1.0 - beta_two) * gradient * gradient
    updated = current - learn_rate * moment_one_new / (jnp.sqrt(moment_two_new) + adam_epsilon)
    return (updated, moment_one_new, moment_two_new)


def spread_pair(key_part, value_part, head_slot, key_width):
    holder = jnp.zeros((key_part.shape[0], 2 * key_width), jnp.float32)
    holder = lax.dynamic_update_slice_in_dim(holder, key_part, head_slot * key_part.shape[1], 1)
    return lax.dynamic_update_slice_in_dim(
        holder, value_part, key_width + head_slot * key_part.shape[1], 1
    )


def on_device(
    frozen_queries,
    key_value_rows,
    output_gradient,
    inputs,
    adapter_down,
    down_first_moment,
    down_second_moment,
    adapter_up,
    up_first_moment,
    up_second_moment,
    rank_keep_mask,
    group_length,
    group_shift,
):
    tokens_here = frozen_queries.shape[0]
    ctx_count = lax.axis_size("ctx")
    ctx_place = lax.axis_index("ctx")
    head_place = lax.axis_index("head")
    reach = min(8, ctx_count // 2)
    heads_here = frozen_queries.shape[1] // HEAD_SIZE
    group_heads = LOCAL_HEADS // KVH
    kv_head = head_place * heads_here // group_heads
    seq_total = tokens_here * ctx_count
    key_width = KVH * HEAD_SIZE
    down_keep_mask = rank_keep_mask[0].astype(jnp.float32)
    down_full, up_full = (
        lax.all_gather(adapter_down.astype(jnp.bfloat16), "ctx", axis=0, tiled=True),
        lax.all_gather(adapter_up.astype(jnp.bfloat16), "ctx", axis=0, tiled=True),
    )
    masked_up_factor = up_full * rank_keep_mask[1][:, None].astype(jnp.bfloat16)
    contract_last = (((1,), (1,)), ((), ()))
    contract_first = (((0,), (0,)), ((), ()))
    projected = lax.psum(
        lax.dot_general(
            inputs, down_full, contract_last, preferred_element_type=jnp.float32
        ).astype(jnp.bfloat16),
        "head",
    ).astype(jnp.float32)
    masked_projection = (projected * down_keep_mask[None, :]).astype(jnp.bfloat16)
    query_values = (
        frozen_queries.astype(jnp.float32)
        + adapter_scale
        * jnp.dot(masked_projection, masked_up_factor, preferred_element_type=jnp.float32)
    ).astype(jnp.bfloat16)
    key_own = lax.dynamic_slice_in_dim(key_value_rows, kv_head * HEAD_SIZE, HEAD_SIZE, 1)
    value_own = lax.dynamic_slice_in_dim(
        key_value_rows, key_width + kv_head * HEAD_SIZE, HEAD_SIZE, 1
    )
    pair_own = jnp.concatenate([key_own, value_own], 1)
    within = jnp.arange(tokens_here, dtype=jnp.int32)
    query_place = ctx_place * tokens_here + within
    offset_here = group_shift[kv_head]
    group_here = group_length[kv_head]
    query_rolled = (query_place - offset_here) % seq_total
    query_group = query_rolled // group_here
    score_scale = 1.0 / math.sqrt(HEAD_SIZE)
    query_heads = query_values.reshape(tokens_here, heads_here, HEAD_SIZE)
    grad_heads = output_gradient.reshape(tokens_here, heads_here, HEAD_SIZE)

    def tile_scores(pair_rows, distance):
        source = (ctx_place - distance + ctx_count) % ctx_count
        key_rolled = (source * tokens_here + within - offset_here) % seq_total
        allowed = (query_group[:, None] == (key_rolled // group_here)[None, :]) & (
            key_rolled[None, :] <= query_rolled[:, None]
        )
        scores = (
            jnp.einsum(
                "qhd,kd->hqk",
                query_heads,
                pair_rows[:, :HEAD_SIZE],
                preferred_element_type=jnp.float32,
            )
            * score_scale
        )
        return jnp.where(allowed[None], scores, -1e30)

    def stats_step(carry, pair_rows, distance):
        running_max, running_total = carry
        scores = tile_scores(pair_rows, distance)
        new_max = jnp.maximum(running_max, jnp.max(scores, -1, keepdims=True))
        running_total = running_total * jnp.exp(running_max - new_max) + jnp.sum(
            jnp.exp(scores - new_max), -1, keepdims=True
        )
        return (new_max, running_total)

    start_max = jnp.full((heads_here, tokens_here, 1), -1e30, jnp.float32)
    start_total = jnp.zeros((heads_here, tokens_here, 1), jnp.float32)
    start_stack = jnp.zeros((reach + 1, tokens_here, 2 * HEAD_SIZE), jnp.bfloat16)

    def first_turn(distance, state):
        held, stack, stats = state
        stack = lax.dynamic_update_index_in_dim(stack, held, distance, 0)
        stats = stats_step(stats, held, distance)
        held = shifted(held, "ctx", 1)
        return (held, stack, stats)

    held, stack, stats = lax.fori_loop(
        0, reach, first_turn, (pair_own, start_stack, (start_max, start_total))
    )
    stack = lax.dynamic_update_index_in_dim(stack, held, reach, 0)
    row_max, total = stats_step(stats, held, reach)

    def weights_of(scores):
        return jnp.exp(scores - row_max) / total

    def out_step(carry, pair_rows, distance):
        out_sum, dot_sum = carry
        weights = weights_of(tile_scores(pair_rows, distance))
        weights_half = weights.astype(jnp.bfloat16)
        out_sum = out_sum + jnp.einsum(
            "hqk,kd->qhd",
            weights_half,
            pair_rows[:, HEAD_SIZE:],
            preferred_element_type=jnp.float32,
        )
        grad_weights = jnp.einsum(
            "qhd,kd->hqk", grad_heads, pair_rows[:, HEAD_SIZE:], preferred_element_type=jnp.float32
        )
        dot_sum = dot_sum + jnp.sum(weights * grad_weights, -1, keepdims=True)
        return (out_sum, dot_sum)

    start_out = (
        jnp.zeros((tokens_here, heads_here, HEAD_SIZE), jnp.float32),
        jnp.zeros((heads_here, tokens_here, 1), jnp.float32),
    )

    def second_kept(distance, inner):
        return out_step(inner, lax.dynamic_index_in_dim(stack, distance, 0, False), distance)

    out_sum, row_dots = lax.fori_loop(0, reach + 1, second_kept, start_out)
    attention_out = out_sum.astype(jnp.bfloat16).reshape(tokens_here, heads_here * HEAD_SIZE)

    def grad_tile(pair_rows, distance):
        weights = weights_of(tile_scores(pair_rows, distance))
        weights_half = weights.astype(jnp.bfloat16)
        grad_weights = jnp.einsum(
            "qhd,kd->hqk", grad_heads, pair_rows[:, HEAD_SIZE:], preferred_element_type=jnp.float32
        )
        grad_scores = (weights * (grad_weights - row_dots)).astype(jnp.bfloat16)
        query_part = jnp.einsum(
            "hqk,kd->qhd", grad_scores, pair_rows[:, :HEAD_SIZE], preferred_element_type=jnp.float32
        )
        key_part = score_scale * jnp.einsum(
            "hqk,qhd->kd", grad_scores, query_heads, preferred_element_type=jnp.float32
        )
        value_part = jnp.einsum(
            "hqk,qhd->kd", weights_half, grad_heads, preferred_element_type=jnp.float32
        )
        return (query_part, jnp.concatenate([key_part, value_part], 1))

    start_query = jnp.zeros((tokens_here, heads_here, HEAD_SIZE), jnp.float32)
    start_pair = jnp.zeros((tokens_here, 2 * HEAD_SIZE), jnp.float32)

    def third_kept(index, state):
        grads_held, query_sum = state
        distance = reach - index
        query_part, pair_part = grad_tile(
            lax.dynamic_index_in_dim(stack, distance, 0, False), distance
        )
        grads_held = shifted((grads_held + pair_part).astype(jnp.bfloat16), "ctx", -1).astype(
            jnp.float32
        )
        return (grads_held, query_sum + query_part)

    grads_held, query_sum = lax.fori_loop(0, reach, third_kept, (start_pair, start_query))
    query_part, pair_part = grad_tile(pair_own, 0)
    query_sum = query_sum + query_part
    pair_total = grads_held + pair_part
    query_gradient = (
        (score_scale * query_sum).astype(jnp.bfloat16).reshape(tokens_here, heads_here * HEAD_SIZE)
    )
    holder = spread_pair(pair_total[:, :HEAD_SIZE], pair_total[:, HEAD_SIZE:], kv_head, key_width)
    kv_grad = lax.psum_scatter(
        holder.astype(jnp.bfloat16), "head", scatter_dimension=1, tiled=True
    ).astype(jnp.float32)
    projection_backward = lax.psum(
        lax.dot_general(
            query_gradient, masked_up_factor, contract_last, preferred_element_type=jnp.float32
        ).astype(jnp.bfloat16),
        "head",
    ).astype(jnp.float32)
    rank_product = (projection_backward * down_keep_mask[None, :] * adapter_scale).astype(
        jnp.bfloat16
    )
    part_down = lax.dot_general(
        rank_product, inputs, contract_first, preferred_element_type=jnp.float32
    )
    partial_up = adapter_scale * lax.dot_general(
        masked_projection, query_gradient, contract_first, preferred_element_type=jnp.float32
    )
    local_rows = adapter_down.shape[0]
    sum_down, sum_up = lax.psum((part_down, partial_up), "ctx")
    down_gradient = lax.dynamic_slice_in_dim(sum_down, ctx_place * local_rows, local_rows, 0)
    up_gradient = lax.dynamic_slice_in_dim(sum_up, ctx_place * local_rows, local_rows, 0)
    keep_rows = lax.dynamic_slice_in_dim(
        rank_keep_mask[1], ctx_place * local_rows, local_rows, 0
    ).astype(jnp.float32)
    up_gradient = keep_rows[:, None] * up_gradient
    updated_down, updated_down_first, updated_down_second = adam_update(
        adapter_down, down_first_moment, down_second_moment, down_gradient
    )
    updated_up, updated_up_first, updated_up_second = adam_update(
        adapter_up, up_first_moment, up_second_moment, up_gradient
    )
    return (
        attention_out,
        query_gradient,
        kv_grad,
        updated_down,
        updated_down_first,
        updated_down_second,
        updated_up,
        updated_up_first,
        updated_up_second,
    )


VMEM_GRANT = 62 * 1024 * 1024
CONTRACT_LAST = (((1,), (1,)), ((), ()))
CONTRACT_FIRST = (((0,), (0,)), ((), ()))


def matmul(left, right, dims=(((1,), (0,)), ((), ()))):
    return lax.dot_general(left, right, dims, preferred_element_type=jnp.float32)


def remote(source, target, send_sem, recv_sem, device):
    return pltpu.make_async_remote_copy(
        src_ref=source,
        dst_ref=target,
        send_sem=send_sem,
        recv_sem=recv_sem,
        device_id=device,
        device_id_type=pl.DeviceIdType.MESH,
    )


def layer_body(
    ctx_count,
    ready,
    frozen_ref,
    rows_ref,
    cotangent_ref,
    inputs_ref,
    down_ref,
    down_one_ref,
    down_two_ref,
    up_ref,
    up_one_ref,
    up_two_ref,
    mask_ref,
    length_ref,
    shift_ref,
    out_ref,
    query_grad_ref,
    kv_grad_ref,
    new_down_ref,
    new_down_one_ref,
    new_down_two_ref,
    new_up_ref,
    new_up_one_ref,
    new_up_two_ref,
    factors,
    down_full,
    up_full,
    pairs,
    proj_parts,
    rank_parts,
    weight_rows,
    score_rows,
    query_columns,
    grad_columns,
    own_part,
    core_send,
    core_parts,
    owner_send,
    owner_parts,
    beside_parts,
    sum_send,
    sum_parts,
    sum_beside,
    send_sems,
    factor_sems,
    pair_sems,
    proj_sems,
    rank_sems,
    core_sems,
    owner_sems,
    beside_sems,
    sum_sems,
    sum_beside_sems,
):
    tokens = frozen_ref.shape[0]
    half = tokens // 2
    heads = frozen_ref.shape[1] // HEAD_SIZE
    reach = pairs.shape[0] - 1
    head_count = proj_parts.shape[0]
    local_rows = down_ref.shape[0]
    down_half = down_ref.shape[1] // 2
    up_half = up_ref.shape[1] // 2
    seq_total = tokens * ctx_count
    key_width = KVH * HEAD_SIZE
    score_scale = 1.0 / math.sqrt(HEAD_SIZE)
    place = lax.axis_index("ctx")
    lane = lax.axis_index("head")
    chip = lane // 2
    core = lane % 2
    odd = place % 2
    beside = place + 1 - 2 * odd
    other_core = lane + 1 - 2 * core
    final_lane = core * 2 + chip
    crossing = chip != core
    used = [0]
    sent = []

    def next_sem():
        used[0] += 1
        return send_sems.at[used[0] - 1]

    def away(steps):
        return lax.rem(place + steps + ctx_count, ctx_count)

    def send(source, target, recv_sem, device, when=None):
        copy = remote(source, target, next_sem(), recv_sem, device)
        if when is None:
            copy.start()
        else:
            pl.when(when)(copy.start)
        sent.append((copy, when))

    def arrived(target, recv_sem):
        remote(target, target, send_sems.at[0], recv_sem, (place, lane)).wait_recv()

    barrier = pltpu.get_barrier_semaphore()

    def greet(device):
        pl.semaphore_signal(
            barrier, inc=1, device_id=device, device_id_type=pl.DeviceIdType.MESH
        )

    for steps in range(1, ctx_count):
        greet((away(steps), lane))
    for steps in range(1, head_count):
        greet((place, lax.rem(lane + steps, head_count)))

    @pl.when(crossing)
    def _():
        for steps in range(1, ctx_count):
            greet((away(steps), final_lane))

    ready(4, 7, 1)
    own_down = down_ref[...]
    own_up = up_ref[...]
    factors[place] = jnp.concatenate(
        [
            jnp.concatenate([own_down[:, :down_half], own_down[:, down_half:]], 0),
            jnp.concatenate([own_up[:, :up_half], own_up[:, up_half:]], 0),
        ],
        1,
    ).astype(jnp.bfloat16)
    key_start = pl.multiple_of(chip * HEAD_SIZE, HEAD_SIZE)
    pairs[0, :, :HEAD_SIZE] = rows_ref[:, pl.ds(key_start, HEAD_SIZE)]
    pairs[0, :, HEAD_SIZE:] = rows_ref[:, pl.ds(key_width + key_start, HEAD_SIZE)]

    straight_peers = ctx_count + head_count - 2

    @pl.when(crossing)
    def _():
        pl.semaphore_wait(barrier, straight_peers + ctx_count - 1)

    @pl.when(jnp.logical_not(crossing))
    def _():
        pl.semaphore_wait(barrier, straight_peers)

    def send_factors(owner, device_place):
        send(
            factors.at[owner], factors.at[owner], factor_sems.at[owner], (device_place, lane)
        )

    half_start = pl.multiple_of(core * half, half)

    def pair_half(slot, start):
        return pairs.at[slot, pl.ds(start, half)]

    def send_pair(slot, new_slot, device, when=None):
        send(
            pair_half(slot, half_start),
            pair_half(new_slot, half_start),
            pair_sems.at[new_slot, core],
            device,
            when,
        )

    for steps in range(2, ctx_count, 2):
        send_factors(place, away(steps))
    send_factors(place, beside)
    send_pair(0, 2, (away(2), lane))
    send_pair(0, 4, (away(4), lane))
    send_pair(0, 1, (beside, lane), odd == 0)
    for steps in range(2, ctx_count, 2):
        owner = away(steps)
        arrived(factors.at[owner], factor_sems.at[owner])
        send_factors(owner, beside)

    core_device = (place, other_core)
    arrived(pair_half(2, half_start), pair_sems.at[2, core])
    send_pair(2, 3, (beside, lane), odd == 0)
    send_pair(2, 1, (beside, lane), odd == 1)
    send_pair(2, 2, core_device)
    arrived(pair_half(4, half_start), pair_sems.at[4, core])
    send_pair(4, 3, (beside, lane), odd == 1)
    send_pair(4, 4, core_device)

    for steps in range(0, ctx_count, 2):
        owner = lax.rem(beside + steps, ctx_count)
        arrived(factors.at[owner], factor_sems.at[owner])

    ready(10, 3, 2)
    mask_rows = mask_ref[...].astype(jnp.float32)
    rank_all = mask_rows.shape[1]
    diagonal = lax.broadcasted_iota(jnp.int32, (rank_all, rank_all), 0) == (
        lax.broadcasted_iota(jnp.int32, (rank_all, rank_all), 1)
    )

    def column(row):
        return jnp.sum(jnp.where(diagonal, row, 0.0), 1, keepdims=True)

    down_keep = column(mask_rows[0:1])
    up_keep = column(mask_rows[1:2])
    for owner in range(ctx_count):
        block = factors[owner].astype(jnp.float32)
        rows = slice(owner * local_rows, (owner + 1) * local_rows)
        down_full[rows, :down_half] = block[:local_rows, :down_half]
        down_full[rows, down_half:] = block[local_rows:, :down_half]
        up_full[rows, :up_half] = block[:local_rows, down_half:]
        up_full[rows, up_half:] = block[local_rows:, down_half:]
    masked_up = (up_full[...] * up_keep).astype(jnp.bfloat16)
    proj_parts[lane] = matmul(
        down_full[...].astype(jnp.bfloat16), inputs_ref[...], CONTRACT_LAST
    ).astype(jnp.bfloat16)

    def send_to_heads(parts, sems):
        for steps in range(1, head_count):
            send(
                parts.at[lane],
                parts.at[lane],
                sems.at[lane],
                (place, lax.rem(lane + steps, head_count)),
            )

    def sum_of_heads(parts, sems):
        for steps in range(1, head_count):
            source = lax.rem(lane + steps, head_count)
            arrived(parts.at[source], sems.at[source])
        total = parts[0].astype(jnp.float32)
        for source in range(1, head_count):
            total = total + parts[source].astype(jnp.float32)
        return total

    send_to_heads(proj_parts, proj_sems)
    for slot in (1, 3):
        arrived(pair_half(slot, half_start), pair_sems.at[slot, core])
        send_pair(slot, slot, core_device)
    other_start = pl.multiple_of((1 - core) * half, half)
    for slot in range(1, reach + 1):
        arrived(pair_half(slot, other_start), pair_sems.at[slot, 1 - core])
    for head in range(heads):
        grad_columns[:, head * tokens : (head + 1) * tokens] = (
            cotangent_ref[:, head * HEAD_SIZE : (head + 1) * HEAD_SIZE].astype(jnp.float32).T
        ).astype(jnp.bfloat16)

    ready(11, 12, 0)
    length = length_ref[chip]
    first_rolled = lax.rem(place * tokens - shift_ref[chip] + seq_total, seq_total)
    first_inside = lax.rem(first_rolled, length)
    query_index = lax.broadcasted_iota(jnp.int32, (tokens, 1), 0)
    inside = first_inside + query_index
    inside = jnp.where(inside >= length, inside - length, inside)
    rolled = first_rolled + query_index
    inside = jnp.where(rolled >= seq_total, rolled - seq_total, inside)
    gap = lax.broadcasted_iota(jnp.int32, (tokens, tokens), 0) - lax.broadcasted_iota(
        jnp.int32, (tokens, tokens), 1
    )
    lower = gap >= 0
    allowed = [jnp.where(lower, gap, gap + reach * tokens) <= inside]
    for slot in range(1, reach):
        allowed.append(gap + slot * tokens <= inside)

    masked_proj = (sum_of_heads(proj_parts, proj_sems) * (down_keep * up_keep)).astype(
        jnp.bfloat16
    )
    span = (reach + 1) * tokens
    all_keys = pairs[:, :, :HEAD_SIZE].reshape(span, HEAD_SIZE)
    all_values = pairs[:, :, HEAD_SIZE:].reshape(span, HEAD_SIZE)

    def tiles_of(product):
        first = jnp.where(lower, product[:, :tokens], product[:, reach * tokens :])
        return [first] + [
            product[:, slot * tokens : (slot + 1) * tokens] for slot in range(1, reach)
        ]

    def spread(tiles):
        nothing = jnp.zeros_like(tiles[0])
        return jnp.concatenate(
            [jnp.where(lower, tiles[0], nothing)]
            + tiles[1:]
            + [jnp.where(lower, nothing, tiles[0])],
            1,
        ).astype(jnp.bfloat16)

    for head in range(heads):
        columns = slice(head * HEAD_SIZE, (head + 1) * HEAD_SIZE)
        rows = slice(head * tokens, (head + 1) * tokens)
        query = (
            frozen_ref[:, columns].astype(jnp.float32)
            + adapter_scale * matmul(masked_proj, masked_up[:, columns], CONTRACT_FIRST)
        )
        query_columns[:, rows] = query.astype(jnp.bfloat16).astype(jnp.float32).T.astype(
            jnp.bfloat16
        )
        query = query.astype(jnp.bfloat16)
        scores = [
            jnp.where(keep, tile * score_scale, -1e30)
            for keep, tile in zip(allowed, tiles_of(matmul(query, all_keys, CONTRACT_LAST)))
        ]
        row_max = jnp.max(
            jnp.maximum(jnp.maximum(scores[0], scores[1]), jnp.maximum(scores[2], scores[3])),
            1,
            keepdims=True,
        )
        powers = [jnp.exp(tile - row_max) for tile in scores]
        total = jnp.sum(powers[0] + powers[1] + powers[2] + powers[3], 1, keepdims=True)
        inverse = 1.0 / total
        weights = [tile * inverse for tile in powers]
        grad_weights = tiles_of(matmul(cotangent_ref[:, columns], all_values, CONTRACT_LAST))
        products = [tile * grad for tile, grad in zip(weights, grad_weights)]
        row_dots = jnp.sum(
            products[0] + products[1] + products[2] + products[3], 1, keepdims=True
        )
        grad_scores = spread(
            [tile * (grad - row_dots) for tile, grad in zip(weights, grad_weights)]
        )
        weights_half = spread(weights)
        weight_rows[rows, :] = weights_half
        score_rows[rows, :] = grad_scores
        out_ref[:, columns] = matmul(weights_half, all_values).astype(jnp.bfloat16)
        query_grad_ref[:, columns] = (score_scale * matmul(grad_scores, all_keys)).astype(
            jnp.bfloat16
        )

    query_grad = query_grad_ref[...]
    rank_parts[lane] = matmul(masked_up, query_grad, CONTRACT_LAST).astype(jnp.bfloat16)
    send_to_heads(rank_parts, rank_sems)

    slots = (3, 1, 4, 2, 0)
    for slot in slots:
        keys = slice(slot * tokens, (slot + 1) * tokens)
        key_part = score_scale * matmul(query_columns[...], score_rows[:, keys])
        value_part = matmul(grad_columns[...], weight_rows[:, keys])
        core_send[slot] = jnp.where(core == 0, value_part, key_part).astype(jnp.bfloat16)
        own_part[slot] = jnp.where(core == 0, key_part, value_part)
        send(core_send.at[slot], core_parts.at[slot], core_sems.at[slot], core_device)

    up_sum = adapter_scale * matmul(masked_proj, query_grad)

    def chip_sum(slot):
        arrived(core_parts.at[slot], core_sems.at[slot])
        return own_part[slot] + core_parts[slot].astype(jnp.float32)

    for index, slot in ((1, 3), (0, 1)):
        owner_send[slot] = chip_sum(slot).astype(jnp.bfloat16)
        send(
            owner_send.at[slot],
            beside_parts.at[index],
            beside_sems.at[index],
            (beside, lane),
        )

    rank_product = (
        sum_of_heads(rank_parts, rank_sems) * (down_keep * adapter_scale)
    ).astype(jnp.bfloat16)
    down_sum = matmul(rank_product, inputs_ref[...])
    for owner in range(ctx_count):
        rows = slice(owner * local_rows, (owner + 1) * local_rows)
        sum_send[owner] = jnp.concatenate(
            [
                jnp.concatenate([down_sum[rows, :down_half], down_sum[rows, down_half:]], 0),
                jnp.concatenate([up_sum[rows, :up_half], up_sum[rows, up_half:]], 0),
            ],
            1,
        ).astype(jnp.bfloat16)
    pair_count = ctx_count // 2
    pair_place = place // 2

    def pair_away(steps):
        return lax.rem(pair_place + steps + pair_count, pair_count)

    for steps in range(1, pair_count + 1):
        owner_pair = pair_away(steps)
        send(
            sum_send.at[2 * owner_pair + 1 - odd],
            sum_beside.at[owner_pair],
            sum_beside_sems.at[owner_pair],
            (beside, lane),
        )

    arrived(beside_parts.at[1], beside_sems.at[1])
    far_extra = beside_parts[1].astype(jnp.float32)
    owner_send[4] = (chip_sum(4) + jnp.where(odd == 1, far_extra, 0.0)).astype(jnp.bfloat16)
    send(
        owner_send.at[4], owner_parts.at[2], owner_sems.at[2], (away(-4), final_lane)
    )
    arrived(beside_parts.at[0], beside_sems.at[0])
    near_extra = beside_parts[0].astype(jnp.float32)
    owner_send[2] = (chip_sum(2) + jnp.where(odd == 1, near_extra, far_extra)).astype(
        jnp.bfloat16
    )
    send(
        owner_send.at[2], owner_parts.at[1], owner_sems.at[1], (away(-2), final_lane)
    )
    owner_send[0] = (chip_sum(0) + jnp.where(odd == 1, 0.0, near_extra)).astype(jnp.bfloat16)
    send(
        owner_send.at[0], owner_parts.at[0], owner_sems.at[0], (place, final_lane), crossing
    )

    for steps in range(1, pair_count):
        owner_pair = pair_away(steps)
        owner = 2 * owner_pair + odd
        arrived(sum_beside.at[owner_pair], sum_beside_sems.at[owner_pair])
        sum_send[owner] = (
            sum_send[owner].astype(jnp.float32) + sum_beside[owner_pair].astype(jnp.float32)
        ).astype(jnp.bfloat16)
        send(
            sum_send.at[owner],
            sum_parts.at[pair_place],
            sum_sems.at[pair_place],
            (owner, lane),
        )
    arrived(sum_beside.at[pair_place], sum_beside_sems.at[pair_place])
    gradient = sum_send[place].astype(jnp.float32) + sum_beside[pair_place].astype(jnp.float32)
    for steps in range(1, pair_count):
        source = pair_away(-steps)
        arrived(sum_parts.at[source], sum_sems.at[source])
        gradient = gradient + sum_parts[source].astype(jnp.float32)
    down_gradient = jnp.concatenate(
        [gradient[:local_rows, :down_half], gradient[local_rows:, :down_half]], 1
    )
    up_gradient = jnp.concatenate(
        [gradient[:local_rows, down_half:], gradient[local_rows:, down_half:]], 1
    )
    ready(5, 6, 8, 9)
    new_down_ref[...], new_down_one_ref[...], new_down_two_ref[...] = adam_update(
        own_down, down_one_ref[...], down_two_ref[...], down_gradient
    )
    new_up_ref[...], new_up_one_ref[...], new_up_two_ref[...] = adam_update(
        own_up, up_one_ref[...], up_two_ref[...], up_gradient
    )

    @pl.when(crossing)
    def _():
        arrived(owner_parts.at[0], owner_sems.at[0])

    @pl.when(jnp.logical_not(crossing))
    def _():
        owner_parts[0] = owner_send[0]

    part_sum = owner_parts[0].astype(jnp.float32)
    for slot in range(1, reach // 2 + 1):
        arrived(owner_parts.at[slot], owner_sems.at[slot])
        part_sum = part_sum + owner_parts[slot].astype(jnp.float32)
    kv_grad_ref[...] = part_sum.T

    for copy, when in sent:
        if when is None:
            copy.wait_send()
        else:
            pl.when(when)(copy.wait_send)


def fused_kernel(ctx_count, *refs):
    operands, results, scratch = refs[:13], refs[13:22], refs[22:]
    local, local_sems = scratch[-14:-1], scratch[-1]
    loads = [
        pltpu.make_async_copy(operand, copy, local_sems.at[index])
        for index, (operand, copy) in enumerate(zip(operands, local))
    ]
    for index in (4, 7, 1, 3, 10, 2, 0, 11, 12, 5, 6, 8, 9):
        loads[index].start()

    def ready(*indices):
        for index in indices:
            loads[index].wait()

    layer_body(ctx_count, ready, *local, *results, *scratch[:-14])


def publish_kernel(*refs):
    count = len(refs) // 2
    copies = [
        pltpu.make_async_copy(refs[index], refs[count + index], refs[-1].at[index])
        for index in range(count)
    ]
    for copy in copies:
        copy.start()
    for copy in copies:
        copy.wait()


def publish(values):
    return pl.pallas_call(
        publish_kernel,
        out_shape=[jax.ShapeDtypeStruct(value.shape, value.dtype) for value in values],
        in_specs=[pl.BlockSpec(memory_space=pl.ANY)] * len(values),
        out_specs=[pl.BlockSpec(memory_space=pltpu.HBM)] * len(values),
        scratch_shapes=[pltpu.SemaphoreType.DMA((len(values),))],
        compiler_params=pltpu.CompilerParams(vmem_limit_bytes=VMEM_GRANT),
    )(*values)


def fused(*args):
    frozen, rows, _, inputs, down, _, _, up = args[:8]
    ctx_count = lax.axis_size("ctx")
    head_count = lax.axis_size("head")
    reach = min(8, ctx_count // 2)
    tokens = frozen.shape[0]
    heads = frozen.shape[1] // HEAD_SIZE
    local_rows = down.shape[0]
    rank_all = local_rows * ctx_count
    block = (2 * local_rows, (down.shape[1] + up.shape[1]) // 2)
    half_type, full_type = jnp.bfloat16, jnp.float32
    in_vmem = pl.BlockSpec(memory_space=pltpu.VMEM)
    in_hbm = pl.BlockSpec(memory_space=pltpu.HBM)
    shapes = [
        (frozen.shape, half_type),
        (frozen.shape, half_type),
        ((tokens, HEAD_SIZE), full_type),
        (down.shape, full_type),
        (down.shape, full_type),
        (down.shape, full_type),
        (up.shape, full_type),
        (up.shape, full_type),
        (up.shape, full_type),
    ]
    return pl.pallas_call(
        functools.partial(fused_kernel, ctx_count),
        out_shape=[jax.ShapeDtypeStruct(shape, kind) for shape, kind in shapes],
        in_specs=[in_hbm] * len(args),
        out_specs=[in_vmem] * 9,
        scratch_shapes=[
            pltpu.VMEM((ctx_count,) + block, half_type),
            pltpu.VMEM((rank_all, down.shape[1]), full_type),
            pltpu.VMEM((rank_all, up.shape[1]), full_type),
            pltpu.VMEM((reach + 1, tokens, 2 * HEAD_SIZE), half_type),
            pltpu.VMEM((head_count, rank_all, tokens), half_type),
            pltpu.VMEM((head_count, rank_all, tokens), half_type),
            pltpu.VMEM((heads * tokens, (reach + 1) * tokens), half_type),
            pltpu.VMEM((heads * tokens, (reach + 1) * tokens), half_type),
            pltpu.VMEM((HEAD_SIZE, heads * tokens), half_type),
            pltpu.VMEM((HEAD_SIZE, heads * tokens), half_type),
            pltpu.VMEM((reach + 1, HEAD_SIZE, tokens), full_type),
            pltpu.VMEM((reach + 1, HEAD_SIZE, tokens), half_type),
            pltpu.VMEM((reach + 1, HEAD_SIZE, tokens), half_type),
            pltpu.VMEM((reach + 1, HEAD_SIZE, tokens), half_type),
            pltpu.VMEM((reach // 2 + 1, HEAD_SIZE, tokens), half_type),
            pltpu.VMEM((2, HEAD_SIZE, tokens), half_type),
            pltpu.VMEM((ctx_count,) + block, half_type),
            pltpu.VMEM((ctx_count // 2,) + block, half_type),
            pltpu.VMEM((ctx_count // 2,) + block, half_type),
            pltpu.SemaphoreType.DMA((64,)),
            pltpu.SemaphoreType.DMA((ctx_count,)),
            pltpu.SemaphoreType.DMA((reach + 1, 2)),
            pltpu.SemaphoreType.DMA((head_count,)),
            pltpu.SemaphoreType.DMA((head_count,)),
            pltpu.SemaphoreType.DMA((reach + 1,)),
            pltpu.SemaphoreType.DMA((reach // 2 + 1,)),
            pltpu.SemaphoreType.DMA((2,)),
            pltpu.SemaphoreType.DMA((ctx_count // 2,)),
            pltpu.SemaphoreType.DMA((ctx_count // 2,)),
        ]
        + [pltpu.VMEM(arg.shape, arg.dtype) for arg in args[:11]]
        + [pltpu.SMEM(arg.shape, arg.dtype) for arg in args[11:]]
        + [pltpu.SemaphoreType.DMA((len(args),))],
        compiler_params=pltpu.CompilerParams(
            collective_id=0, has_side_effects=True, vmem_limit_bytes=VMEM_GRANT
        ),
    )(*args)


def on_any_mesh(*args):
    fits = (
        min(8, lax.axis_size("ctx") // 2) == 4
        and lax.axis_size("ctx") % 2 == 0
        and args[4].shape[0] % 8 == 0
        and lax.axis_size("head") == 2 * KVH
    )
    return tuple(publish(fused(*args))) if fits else on_device(*args)


def solution(mesh):
    placed = (
        P("ctx", "head"),
        P("ctx", None),
        P("ctx", "head"),
        P("ctx", "head"),
        P("ctx", "head"),
        P("ctx", "head"),
        P("ctx", "head"),
        P("ctx", "head"),
        P("ctx", "head"),
        P("ctx", "head"),
        P(),
        P(),
        P(),
    )
    return jax.shard_map(
        on_any_mesh,
        mesh=mesh,
        in_specs=placed,
        out_specs=(
            P("ctx", "head"),
            P("ctx", "head"),
            P("ctx", "head"),
            P("ctx", "head"),
            P("ctx", "head"),
            P("ctx", "head"),
            P("ctx", "head"),
            P("ctx", "head"),
            P("ctx", "head"),
        ),
        check_vma=False,
    )
```

```python
import functools
import math

import jax
import jax.numpy as jnp
from jax import lax
from jax.experimental import pallas as pl
from jax.experimental.pallas import tpu as pltpu
from jax.sharding import PartitionSpec as P

LOCAL_HEADS = 16
KVH = 2
HEAD_SIZE = 128


adapter_scale = 0.25
beta_one = 0.9
beta_two = 0.999
learn_rate = 0.01
adam_epsilon = 1e-08


def shifted(value, axis, steps):
    count = lax.axis_size(axis)
    pairs = [(source, (source + steps) % count) for source in range(count)]
    return lax.ppermute(value, axis, pairs)


def adam_update(current, moment_one, moment_two, gradient):
    moment_one_new = beta_one * moment_one + (1.0 - beta_one) * gradient
    moment_two_new = beta_two * moment_two + (1.0 - beta_two) * gradient * gradient
    updated = current - learn_rate * moment_one_new / (jnp.sqrt(moment_two_new) + adam_epsilon)
    return (updated, moment_one_new, moment_two_new)


def spread_pair(key_part, value_part, head_slot, key_width):
    holder = jnp.zeros((key_part.shape[0], 2 * key_width), jnp.float32)
    holder = lax.dynamic_update_slice_in_dim(holder, key_part, head_slot * key_part.shape[1], 1)
    return lax.dynamic_update_slice_in_dim(
        holder, value_part, key_width + head_slot * key_part.shape[1], 1
    )


def on_device(
    frozen_queries,
    key_value_rows,
    output_gradient,
    inputs,
    adapter_down,
    down_first_moment,
    down_second_moment,
    adapter_up,
    up_first_moment,
    up_second_moment,
    rank_keep_mask,
    group_length,
    group_shift,
):
    tokens_here = frozen_queries.shape[0]
    ctx_count = lax.axis_size("ctx")
    ctx_place = lax.axis_index("ctx")
    head_place = lax.axis_index("head")
    reach = min(8, ctx_count // 2)
    heads_here = frozen_queries.shape[1] // HEAD_SIZE
    group_heads = LOCAL_HEADS // KVH
    kv_head = head_place * heads_here // group_heads
    seq_total = tokens_here * ctx_count
    key_width = KVH * HEAD_SIZE
    down_keep_mask = rank_keep_mask[0].astype(jnp.float32)
    down_full, up_full = (
        lax.all_gather(adapter_down.astype(jnp.bfloat16), "ctx", axis=0, tiled=True),
        lax.all_gather(adapter_up.astype(jnp.bfloat16), "ctx", axis=0, tiled=True),
    )
    masked_up_factor = up_full * rank_keep_mask[1][:, None].astype(jnp.bfloat16)
    contract_last = (((1,), (1,)), ((), ()))
    contract_first = (((0,), (0,)), ((), ()))
    projected = lax.psum(
        lax.dot_general(
            inputs, down_full, contract_last, preferred_element_type=jnp.float32
        ).astype(jnp.bfloat16),
        "head",
    ).astype(jnp.float32)
    masked_projection = (projected * down_keep_mask[None, :]).astype(jnp.bfloat16)
    query_values = (
        frozen_queries.astype(jnp.float32)
        + adapter_scale
        * jnp.dot(masked_projection, masked_up_factor, preferred_element_type=jnp.float32)
    ).astype(jnp.bfloat16)
    key_own = lax.dynamic_slice_in_dim(key_value_rows, kv_head * HEAD_SIZE, HEAD_SIZE, 1)
    value_own = lax.dynamic_slice_in_dim(
        key_value_rows, key_width + kv_head * HEAD_SIZE, HEAD_SIZE, 1
    )
    pair_own = jnp.concatenate([key_own, value_own], 1)
    within = jnp.arange(tokens_here, dtype=jnp.int32)
    query_place = ctx_place * tokens_here + within
    offset_here = group_shift[kv_head]
    group_here = group_length[kv_head]
    query_rolled = (query_place - offset_here) % seq_total
    query_group = query_rolled // group_here
    score_scale = 1.0 / math.sqrt(HEAD_SIZE)
    query_heads = query_values.reshape(tokens_here, heads_here, HEAD_SIZE)
    grad_heads = output_gradient.reshape(tokens_here, heads_here, HEAD_SIZE)

    def tile_scores(pair_rows, distance):
        source = (ctx_place - distance + ctx_count) % ctx_count
        key_rolled = (source * tokens_here + within - offset_here) % seq_total
        allowed = (query_group[:, None] == (key_rolled // group_here)[None, :]) & (
            key_rolled[None, :] <= query_rolled[:, None]
        )
        scores = (
            jnp.einsum(
                "qhd,kd->hqk",
                query_heads,
                pair_rows[:, :HEAD_SIZE],
                preferred_element_type=jnp.float32,
            )
            * score_scale
        )
        return jnp.where(allowed[None], scores, -1e30)

    def stats_step(carry, pair_rows, distance):
        running_max, running_total = carry
        scores = tile_scores(pair_rows, distance)
        new_max = jnp.maximum(running_max, jnp.max(scores, -1, keepdims=True))
        running_total = running_total * jnp.exp(running_max - new_max) + jnp.sum(
            jnp.exp(scores - new_max), -1, keepdims=True
        )
        return (new_max, running_total)

    start_max = jnp.full((heads_here, tokens_here, 1), -1e30, jnp.float32)
    start_total = jnp.zeros((heads_here, tokens_here, 1), jnp.float32)
    start_stack = jnp.zeros((reach + 1, tokens_here, 2 * HEAD_SIZE), jnp.bfloat16)

    def first_turn(distance, state):
        held, stack, stats = state
        stack = lax.dynamic_update_index_in_dim(stack, held, distance, 0)
        stats = stats_step(stats, held, distance)
        held = shifted(held, "ctx", 1)
        return (held, stack, stats)

    held, stack, stats = lax.fori_loop(
        0, reach, first_turn, (pair_own, start_stack, (start_max, start_total))
    )
    stack = lax.dynamic_update_index_in_dim(stack, held, reach, 0)
    row_max, total = stats_step(stats, held, reach)

    def weights_of(scores):
        return jnp.exp(scores - row_max) / total

    def out_step(carry, pair_rows, distance):
        out_sum, dot_sum = carry
        weights = weights_of(tile_scores(pair_rows, distance))
        weights_half = weights.astype(jnp.bfloat16)
        out_sum = out_sum + jnp.einsum(
            "hqk,kd->qhd",
            weights_half,
            pair_rows[:, HEAD_SIZE:],
            preferred_element_type=jnp.float32,
        )
        grad_weights = jnp.einsum(
            "qhd,kd->hqk", grad_heads, pair_rows[:, HEAD_SIZE:], preferred_element_type=jnp.float32
        )
        dot_sum = dot_sum + jnp.sum(weights * grad_weights, -1, keepdims=True)
        return (out_sum, dot_sum)

    start_out = (
        jnp.zeros((tokens_here, heads_here, HEAD_SIZE), jnp.float32),
        jnp.zeros((heads_here, tokens_here, 1), jnp.float32),
    )

    def second_kept(distance, inner):
        return out_step(inner, lax.dynamic_index_in_dim(stack, distance, 0, False), distance)

    out_sum, row_dots = lax.fori_loop(0, reach + 1, second_kept, start_out)
    attention_out = out_sum.astype(jnp.bfloat16).reshape(tokens_here, heads_here * HEAD_SIZE)

    def grad_tile(pair_rows, distance):
        weights = weights_of(tile_scores(pair_rows, distance))
        weights_half = weights.astype(jnp.bfloat16)
        grad_weights = jnp.einsum(
            "qhd,kd->hqk", grad_heads, pair_rows[:, HEAD_SIZE:], preferred_element_type=jnp.float32
        )
        grad_scores = (weights * (grad_weights - row_dots)).astype(jnp.bfloat16)
        query_part = jnp.einsum(
            "hqk,kd->qhd", grad_scores, pair_rows[:, :HEAD_SIZE], preferred_element_type=jnp.float32
        )
        key_part = score_scale * jnp.einsum(
            "hqk,qhd->kd", grad_scores, query_heads, preferred_element_type=jnp.float32
        )
        value_part = jnp.einsum(
            "hqk,qhd->kd", weights_half, grad_heads, preferred_element_type=jnp.float32
        )
        return (query_part, jnp.concatenate([key_part, value_part], 1))

    start_query = jnp.zeros((tokens_here, heads_here, HEAD_SIZE), jnp.float32)
    start_pair = jnp.zeros((tokens_here, 2 * HEAD_SIZE), jnp.float32)

    def third_kept(index, state):
        grads_held, query_sum = state
        distance = reach - index
        query_part, pair_part = grad_tile(
            lax.dynamic_index_in_dim(stack, distance, 0, False), distance
        )
        grads_held = shifted((grads_held + pair_part).astype(jnp.bfloat16), "ctx", -1).astype(
            jnp.float32
        )
        return (grads_held, query_sum + query_part)

    grads_held, query_sum = lax.fori_loop(0, reach, third_kept, (start_pair, start_query))
    query_part, pair_part = grad_tile(pair_own, 0)
    query_sum = query_sum + query_part
    pair_total = grads_held + pair_part
    query_gradient = (
        (score_scale * query_sum).astype(jnp.bfloat16).reshape(tokens_here, heads_here * HEAD_SIZE)
    )
    holder = spread_pair(pair_total[:, :HEAD_SIZE], pair_total[:, HEAD_SIZE:], kv_head, key_width)
    kv_grad = lax.psum_scatter(
        holder.astype(jnp.bfloat16), "head", scatter_dimension=1, tiled=True
    ).astype(jnp.float32)
    projection_backward = lax.psum(
        lax.dot_general(
            query_gradient, masked_up_factor, contract_last, preferred_element_type=jnp.float32
        ).astype(jnp.bfloat16),
        "head",
    ).astype(jnp.float32)
    rank_product = (projection_backward * down_keep_mask[None, :] * adapter_scale).astype(
        jnp.bfloat16
    )
    part_down = lax.dot_general(
        rank_product, inputs, contract_first, preferred_element_type=jnp.float32
    )
    partial_up = adapter_scale * lax.dot_general(
        masked_projection, query_gradient, contract_first, preferred_element_type=jnp.float32
    )
    local_rows = adapter_down.shape[0]
    sum_down, sum_up = lax.psum((part_down, partial_up), "ctx")
    down_gradient = lax.dynamic_slice_in_dim(sum_down, ctx_place * local_rows, local_rows, 0)
    up_gradient = lax.dynamic_slice_in_dim(sum_up, ctx_place * local_rows, local_rows, 0)
    keep_rows = lax.dynamic_slice_in_dim(
        rank_keep_mask[1], ctx_place * local_rows, local_rows, 0
    ).astype(jnp.float32)
    up_gradient = keep_rows[:, None] * up_gradient
    updated_down, updated_down_first, updated_down_second = adam_update(
        adapter_down, down_first_moment, down_second_moment, down_gradient
    )
    updated_up, updated_up_first, updated_up_second = adam_update(
        adapter_up, up_first_moment, up_second_moment, up_gradient
    )
    return (
        attention_out,
        query_gradient,
        kv_grad,
        updated_down,
        updated_down_first,
        updated_down_second,
        updated_up,
        updated_up_first,
        updated_up_second,
    )


VMEM_GRANT = 62 * 1024 * 1024
CONTRACT_LAST = (((1,), (1,)), ((), ()))
CONTRACT_FIRST = (((0,), (0,)), ((), ()))


def matmul(left, right, dims=(((1,), (0,)), ((), ()))):
    return lax.dot_general(left, right, dims, preferred_element_type=jnp.float32)


def remote(source, target, send_sem, recv_sem, device):
    return pltpu.make_async_remote_copy(
        src_ref=source,
        dst_ref=target,
        send_sem=send_sem,
        recv_sem=recv_sem,
        device_id=device,
        device_id_type=pl.DeviceIdType.MESH,
    )


def layer_body(
    ctx_count,
    ready,
    frozen_ref,
    rows_ref,
    cotangent_ref,
    inputs_ref,
    down_ref,
    down_one_ref,
    down_two_ref,
    up_ref,
    up_one_ref,
    up_two_ref,
    mask_ref,
    length_ref,
    shift_ref,
    out_ref,
    query_grad_ref,
    kv_grad_ref,
    new_down_ref,
    new_down_one_ref,
    new_down_two_ref,
    new_up_ref,
    new_up_one_ref,
    new_up_two_ref,
    factors,
    down_full,
    up_full,
    pairs,
    proj_parts,
    rank_parts,
    weight_rows,
    score_rows,
    query_columns,
    grad_columns,
    own_part,
    core_send,
    core_parts,
    owner_send,
    owner_parts,
    beside_parts,
    sum_send,
    sum_parts,
    sum_beside,
    send_sems,
    factor_sems,
    pair_sems,
    proj_sems,
    rank_sems,
    core_sems,
    owner_sems,
    beside_sems,
    sum_sems,
    sum_beside_sems,
):
    tokens = frozen_ref.shape[0]
    half = tokens // 2
    heads = frozen_ref.shape[1] // HEAD_SIZE
    reach = pairs.shape[0] - 1
    head_count = proj_parts.shape[0]
    local_rows = down_ref.shape[0]
    down_half = down_ref.shape[1] // 2
    up_half = up_ref.shape[1] // 2
    seq_total = tokens * ctx_count
    key_width = KVH * HEAD_SIZE
    score_scale = 1.0 / math.sqrt(HEAD_SIZE)
    place = lax.axis_index("ctx")
    lane = lax.axis_index("head")
    chip = lane // 2
    core = lane % 2
    odd = place % 2
    beside = place + 1 - 2 * odd
    other_core = lane + 1 - 2 * core
    final_lane = core * 2 + chip
    crossing = chip != core
    used = [0]
    sent = []

    def next_sem():
        used[0] += 1
        return send_sems.at[used[0] - 1]

    def away(steps):
        return lax.rem(place + steps + ctx_count, ctx_count)

    def send(source, target, recv_sem, device, when=None):
        copy = remote(source, target, next_sem(), recv_sem, device)
        if when is None:
            copy.start()
        else:
            pl.when(when)(copy.start)
        sent.append((copy, when))

    def arrived(target, recv_sem):
        remote(target, target, send_sems.at[0], recv_sem, (place, lane)).wait_recv()

    barrier = pltpu.get_barrier_semaphore()

    def greet(device):
        pl.semaphore_signal(
            barrier, inc=1, device_id=device, device_id_type=pl.DeviceIdType.MESH
        )

    for steps in range(1, ctx_count):
        greet((away(steps), lane))
    for steps in range(1, head_count):
        greet((place, lax.rem(lane + steps, head_count)))

    @pl.when(crossing)
    def _():
        for steps in range(1, ctx_count):
            greet((away(steps), final_lane))

    ready(4, 7, 1)
    own_down = down_ref[...]
    own_up = up_ref[...]
    factors[place] = jnp.concatenate(
        [
            jnp.concatenate([own_down[:, :down_half], own_down[:, down_half:]], 0),
            jnp.concatenate([own_up[:, :up_half], own_up[:, up_half:]], 0),
        ],
        1,
    ).astype(jnp.bfloat16)
    key_start = pl.multiple_of(chip * HEAD_SIZE, HEAD_SIZE)
    pairs[0, :, :HEAD_SIZE] = rows_ref[:, pl.ds(key_start, HEAD_SIZE)]
    pairs[0, :, HEAD_SIZE:] = rows_ref[:, pl.ds(key_width + key_start, HEAD_SIZE)]

    straight_peers = ctx_count + head_count - 2

    @pl.when(crossing)
    def _():
        pl.semaphore_wait(barrier, straight_peers + ctx_count - 1)

    @pl.when(jnp.logical_not(crossing))
    def _():
        pl.semaphore_wait(barrier, straight_peers)

    def send_factors(owner, device_place):
        send(
            factors.at[owner], factors.at[owner], factor_sems.at[owner], (device_place, lane)
        )

    half_start = pl.multiple_of(core * half, half)

    def pair_half(slot, start):
        return pairs.at[slot, pl.ds(start, half)]

    def send_pair(slot, new_slot, device, when=None):
        send(
            pair_half(slot, half_start),
            pair_half(new_slot, half_start),
            pair_sems.at[new_slot, core],
            device,
            when,
        )

    for steps in range(2, ctx_count, 2):
        send_factors(place, away(steps))
    send_factors(place, beside)
    send_pair(0, 2, (away(2), lane))
    send_pair(0, 4, (away(4), lane))
    send_pair(0, 1, (beside, lane), odd == 0)
    for steps in range(2, ctx_count, 2):
        owner = away(steps)
        arrived(factors.at[owner], factor_sems.at[owner])
        send_factors(owner, beside)

    core_device = (place, other_core)
    arrived(pair_half(2, half_start), pair_sems.at[2, core])
    send_pair(2, 3, (beside, lane), odd == 0)
    send_pair(2, 1, (beside, lane), odd == 1)
    send_pair(2, 2, core_device)
    arrived(pair_half(4, half_start), pair_sems.at[4, core])
    send_pair(4, 3, (beside, lane), odd == 1)
    send_pair(4, 4, core_device)

    for steps in range(0, ctx_count, 2):
        owner = lax.rem(beside + steps, ctx_count)
        arrived(factors.at[owner], factor_sems.at[owner])

    ready(10, 3, 2)
    mask_rows = mask_ref[...].astype(jnp.float32)
    rank_all = mask_rows.shape[1]
    diagonal = lax.broadcasted_iota(jnp.int32, (rank_all, rank_all), 0) == (
        lax.broadcasted_iota(jnp.int32, (rank_all, rank_all), 1)
    )

    def column(row):
        return jnp.sum(jnp.where(diagonal, row, 0.0), 1, keepdims=True)

    down_keep = column(mask_rows[0:1])
    up_keep = column(mask_rows[1:2])
    for owner in range(ctx_count):
        block = factors[owner].astype(jnp.float32)
        rows = slice(owner * local_rows, (owner + 1) * local_rows)
        down_full[rows, :down_half] = block[:local_rows, :down_half]
        down_full[rows, down_half:] = block[local_rows:, :down_half]
        up_full[rows, :up_half] = block[:local_rows, down_half:]
        up_full[rows, up_half:] = block[local_rows:, down_half:]
    masked_up = (up_full[...] * up_keep).astype(jnp.bfloat16)
    proj_parts[lane] = matmul(
        down_full[...].astype(jnp.bfloat16), inputs_ref[...], CONTRACT_LAST
    ).astype(jnp.bfloat16)

    def send_to_heads(parts, sems):
        for steps in range(1, head_count):
            send(
                parts.at[lane],
                parts.at[lane],
                sems.at[lane],
                (place, lax.rem(lane + steps, head_count)),
            )

    def sum_of_heads(parts, sems):
        for steps in range(1, head_count):
            source = lax.rem(lane + steps, head_count)
            arrived(parts.at[source], sems.at[source])
        total = parts[0].astype(jnp.float32)
        for source in range(1, head_count):
            total = total + parts[source].astype(jnp.float32)
        return total

    send_to_heads(proj_parts, proj_sems)
    for slot in (1, 3):
        arrived(pair_half(slot, half_start), pair_sems.at[slot, core])
        send_pair(slot, slot, core_device)
    other_start = pl.multiple_of((1 - core) * half, half)
    for slot in range(1, reach + 1):
        arrived(pair_half(slot, other_start), pair_sems.at[slot, 1 - core])
    for head in range(heads):
        grad_columns[:, head * tokens : (head + 1) * tokens] = (
            cotangent_ref[:, head * HEAD_SIZE : (head + 1) * HEAD_SIZE].astype(jnp.float32).T
        ).astype(jnp.bfloat16)

    ready(11, 12, 0)
    length = length_ref[chip]
    first_rolled = lax.rem(place * tokens - shift_ref[chip] + seq_total, seq_total)
    first_inside = lax.rem(first_rolled, length)
    query_index = lax.broadcasted_iota(jnp.int32, (tokens, 1), 0)
    inside = first_inside + query_index
    inside = jnp.where(inside >= length, inside - length, inside)
    rolled = first_rolled + query_index
    inside = jnp.where(rolled >= seq_total, rolled - seq_total, inside)
    gap = lax.broadcasted_iota(jnp.int32, (tokens, tokens), 0) - lax.broadcasted_iota(
        jnp.int32, (tokens, tokens), 1
    )
    lower = gap >= 0
    allowed = [jnp.where(lower, gap, gap + reach * tokens) <= inside]
    for slot in range(1, reach):
        allowed.append(gap + slot * tokens <= inside)

    masked_proj = (sum_of_heads(proj_parts, proj_sems) * (down_keep * up_keep)).astype(
        jnp.bfloat16
    )
    span = (reach + 1) * tokens
    all_keys = pairs[:, :, :HEAD_SIZE].reshape(span, HEAD_SIZE)
    all_values = pairs[:, :, HEAD_SIZE:].reshape(span, HEAD_SIZE)

    def tiles_of(product):
        first = jnp.where(lower, product[:, :tokens], product[:, reach * tokens :])
        return [first] + [
            product[:, slot * tokens : (slot + 1) * tokens] for slot in range(1, reach)
        ]

    def spread(tiles):
        nothing = jnp.zeros_like(tiles[0])
        return jnp.concatenate(
            [jnp.where(lower, tiles[0], nothing)]
            + tiles[1:]
            + [jnp.where(lower, nothing, tiles[0])],
            1,
        ).astype(jnp.bfloat16)

    for head in range(heads):
        columns = slice(head * HEAD_SIZE, (head + 1) * HEAD_SIZE)
        rows = slice(head * tokens, (head + 1) * tokens)
        query = (
            frozen_ref[:, columns].astype(jnp.float32)
            + adapter_scale * matmul(masked_proj, masked_up[:, columns], CONTRACT_FIRST)
        )
        query_columns[:, rows] = query.astype(jnp.bfloat16).astype(jnp.float32).T.astype(
            jnp.bfloat16
        )
        query = query.astype(jnp.bfloat16)
        scores = [
            jnp.where(keep, tile * score_scale, -1e30)
            for keep, tile in zip(allowed, tiles_of(matmul(query, all_keys, CONTRACT_LAST)))
        ]
        row_max = jnp.max(
            jnp.maximum(jnp.maximum(scores[0], scores[1]), jnp.maximum(scores[2], scores[3])),
            1,
            keepdims=True,
        )
        powers = [jnp.exp(tile - row_max) for tile in scores]
        total = jnp.sum(powers[0] + powers[1] + powers[2] + powers[3], 1, keepdims=True)
        inverse = 1.0 / total
        weights = [tile * inverse for tile in powers]
        grad_weights = tiles_of(matmul(cotangent_ref[:, columns], all_values, CONTRACT_LAST))
        products = [tile * grad for tile, grad in zip(weights, grad_weights)]
        row_dots = jnp.sum(
            products[0] + products[1] + products[2] + products[3], 1, keepdims=True
        )
        grad_scores = spread(
            [tile * (grad - row_dots) for tile, grad in zip(weights, grad_weights)]
        )
        weights_half = spread(weights)
        weight_rows[rows, :] = weights_half
        score_rows[rows, :] = grad_scores
        out_ref[:, columns] = matmul(weights_half, all_values).astype(jnp.bfloat16)
        query_grad_ref[:, columns] = (score_scale * matmul(grad_scores, all_keys)).astype(
            jnp.bfloat16
        )

    query_grad = query_grad_ref[...]
    rank_parts[lane] = matmul(masked_up, query_grad, CONTRACT_LAST).astype(jnp.bfloat16)
    send_to_heads(rank_parts, rank_sems)

    slots = (3, 1, 4, 2, 0)
    for slot in slots:
        keys = slice(slot * tokens, (slot + 1) * tokens)
        key_part = score_scale * matmul(query_columns[...], score_rows[:, keys])
        value_part = matmul(grad_columns[...], weight_rows[:, keys])
        core_send[slot] = jnp.where(core == 0, value_part, key_part).astype(jnp.bfloat16)
        own_part[slot] = jnp.where(core == 0, key_part, value_part)
        send(core_send.at[slot], core_parts.at[slot], core_sems.at[slot], core_device)

    up_sum = adapter_scale * matmul(masked_proj, query_grad)

    def chip_sum(slot):
        arrived(core_parts.at[slot], core_sems.at[slot])
        return own_part[slot] + core_parts[slot].astype(jnp.float32)

    for index, slot in ((1, 3), (0, 1)):
        owner_send[slot] = chip_sum(slot).astype(jnp.bfloat16)
        send(
            owner_send.at[slot],
            beside_parts.at[index],
            beside_sems.at[index],
            (beside, lane),
        )

    rank_product = (
        sum_of_heads(rank_parts, rank_sems) * (down_keep * adapter_scale)
    ).astype(jnp.bfloat16)
    down_sum = matmul(rank_product, inputs_ref[...])
    for owner in range(ctx_count):
        rows = slice(owner * local_rows, (owner + 1) * local_rows)
        sum_send[owner] = jnp.concatenate(
            [
                jnp.concatenate([down_sum[rows, :down_half], down_sum[rows, down_half:]], 0),
                jnp.concatenate([up_sum[rows, :up_half], up_sum[rows, up_half:]], 0),
            ],
            1,
        ).astype(jnp.bfloat16)
    pair_count = ctx_count // 2
    pair_place = place // 2

    def pair_away(steps):
        return lax.rem(pair_place + steps + pair_count, pair_count)

    for steps in range(1, pair_count + 1):
        owner_pair = pair_away(steps)
        send(
            sum_send.at[2 * owner_pair + 1 - odd],
            sum_beside.at[owner_pair],
            sum_beside_sems.at[owner_pair],
            (beside, lane),
        )

    arrived(beside_parts.at[1], beside_sems.at[1])
    far_extra = beside_parts[1].astype(jnp.float32)
    owner_send[4] = (chip_sum(4) + jnp.where(odd == 1, far_extra, 0.0)).astype(jnp.bfloat16)
    send(
        owner_send.at[4], owner_parts.at[2], owner_sems.at[2], (away(-4), final_lane)
    )
    arrived(beside_parts.at[0], beside_sems.at[0])
    near_extra = beside_parts[0].astype(jnp.float32)
    owner_send[2] = (chip_sum(2) + jnp.where(odd == 1, near_extra, far_extra)).astype(
        jnp.bfloat16
    )
    send(
        owner_send.at[2], owner_parts.at[1], owner_sems.at[1], (away(-2), final_lane)
    )
    owner_send[0] = (chip_sum(0) + jnp.where(odd == 1, 0.0, near_extra)).astype(jnp.bfloat16)
    send(
        owner_send.at[0], owner_parts.at[0], owner_sems.at[0], (place, final_lane), crossing
    )

    for steps in range(1, pair_count):
        owner_pair = pair_away(steps)
        owner = 2 * owner_pair + odd
        arrived(sum_beside.at[owner_pair], sum_beside_sems.at[owner_pair])
        sum_send[owner] = (
            sum_send[owner].astype(jnp.float32) + sum_beside[owner_pair].astype(jnp.float32)
        ).astype(jnp.bfloat16)
        send(
            sum_send.at[owner],
            sum_parts.at[pair_place],
            sum_sems.at[pair_place],
            (owner, lane),
        )
    arrived(sum_beside.at[pair_place], sum_beside_sems.at[pair_place])
    gradient = sum_send[place].astype(jnp.float32) + sum_beside[pair_place].astype(jnp.float32)
    for steps in range(1, pair_count):
        source = pair_away(-steps)
        arrived(sum_parts.at[source], sum_sems.at[source])
        gradient = gradient + sum_parts[source].astype(jnp.float32)
    down_gradient = jnp.concatenate(
        [gradient[:local_rows, :down_half], gradient[local_rows:, :down_half]], 1
    )
    up_gradient = jnp.concatenate(
        [gradient[:local_rows, down_half:], gradient[local_rows:, down_half:]], 1
    )
    ready(5, 6, 8, 9)
    new_down_ref[...], new_down_one_ref[...], new_down_two_ref[...] = adam_update(
        own_down, down_one_ref[...], down_two_ref[...], down_gradient
    )
    new_up_ref[...], new_up_one_ref[...], new_up_two_ref[...] = adam_update(
        own_up, up_one_ref[...], up_two_ref[...], up_gradient
    )

    @pl.when(crossing)
    def _():
        arrived(owner_parts.at[0], owner_sems.at[0])

    @pl.when(jnp.logical_not(crossing))
    def _():
        owner_parts[0] = owner_send[0]

    part_sum = owner_parts[0].astype(jnp.float32)
    for slot in range(1, reach // 2 + 1):
        arrived(owner_parts.at[slot], owner_sems.at[slot])
        part_sum = part_sum + owner_parts[slot].astype(jnp.float32)
    kv_grad_ref[...] = part_sum.T

    for copy, when in sent:
        if when is None:
            copy.wait_send()
        else:
            pl.when(when)(copy.wait_send)


def fused_kernel(ctx_count, *refs):
    operands, results, scratch = refs[:13], refs[13:22], refs[22:]
    local, local_sems = scratch[-14:-1], scratch[-1]
    loads = [
        pltpu.make_async_copy(operand, copy, local_sems.at[index])
        for index, (operand, copy) in enumerate(zip(operands, local))
    ]
    for index in (4, 7, 1, 3, 10, 2, 0, 11, 12, 5, 6, 8, 9):
        loads[index].start()

    def ready(*indices):
        for index in indices:
            loads[index].wait()

    layer_body(ctx_count, ready, *local, *results, *scratch[:-14])


def publish_kernel(count, *refs):
    values, results, staged = refs[:count], refs[count : 2 * count], refs[2 * count : -1]
    loads = [
        pltpu.make_async_copy(values[index], staged[index], refs[-1].at[0, index])
        for index in range(count)
    ]
    stores = [
        pltpu.make_async_copy(staged[index], results[index], refs[-1].at[1, index])
        for index in range(count)
    ]
    for load in loads:
        load.start()
    for load, store in zip(loads, stores):
        load.wait()
        store.start()
    for store in stores:
        store.wait()


def publish(values):
    count = len(values)
    return pl.pallas_call(
        functools.partial(publish_kernel, count),
        out_shape=[jax.ShapeDtypeStruct(value.shape, value.dtype) for value in values],
        in_specs=[pl.BlockSpec(memory_space=pltpu.HBM)] * count,
        out_specs=[pl.BlockSpec(memory_space=pltpu.HBM)] * count,
        scratch_shapes=[pltpu.VMEM(value.shape, value.dtype) for value in values]
        + [pltpu.SemaphoreType.DMA((2, count))],
        compiler_params=pltpu.CompilerParams(vmem_limit_bytes=VMEM_GRANT),
    )(*values)


def fused(*args):
    frozen, rows, _, inputs, down, _, _, up = args[:8]
    ctx_count = lax.axis_size("ctx")
    head_count = lax.axis_size("head")
    reach = min(8, ctx_count // 2)
    tokens = frozen.shape[0]
    heads = frozen.shape[1] // HEAD_SIZE
    local_rows = down.shape[0]
    rank_all = local_rows * ctx_count
    block = (2 * local_rows, (down.shape[1] + up.shape[1]) // 2)
    half_type, full_type = jnp.bfloat16, jnp.float32
    in_vmem = pl.BlockSpec(memory_space=pltpu.VMEM)
    in_hbm = pl.BlockSpec(memory_space=pltpu.HBM)
    shapes = [
        (frozen.shape, half_type),
        (frozen.shape, half_type),
        ((tokens, HEAD_SIZE), full_type),
        (down.shape, full_type),
        (down.shape, full_type),
        (down.shape, full_type),
        (up.shape, full_type),
        (up.shape, full_type),
        (up.shape, full_type),
    ]
    return pl.pallas_call(
        functools.partial(fused_kernel, ctx_count),
        out_shape=[jax.ShapeDtypeStruct(shape, kind) for shape, kind in shapes],
        in_specs=[in_hbm] * len(args),
        out_specs=[in_vmem] * 9,
        scratch_shapes=[
            pltpu.VMEM((ctx_count,) + block, half_type),
            pltpu.VMEM((rank_all, down.shape[1]), full_type),
            pltpu.VMEM((rank_all, up.shape[1]), full_type),
            pltpu.VMEM((reach + 1, tokens, 2 * HEAD_SIZE), half_type),
            pltpu.VMEM((head_count, rank_all, tokens), half_type),
            pltpu.VMEM((head_count, rank_all, tokens), half_type),
            pltpu.VMEM((heads * tokens, (reach + 1) * tokens), half_type),
            pltpu.VMEM((heads * tokens, (reach + 1) * tokens), half_type),
            pltpu.VMEM((HEAD_SIZE, heads * tokens), half_type),
            pltpu.VMEM((HEAD_SIZE, heads * tokens), half_type),
            pltpu.VMEM((reach + 1, HEAD_SIZE, tokens), full_type),
            pltpu.VMEM((reach + 1, HEAD_SIZE, tokens), half_type),
            pltpu.VMEM((reach + 1, HEAD_SIZE, tokens), half_type),
            pltpu.VMEM((reach + 1, HEAD_SIZE, tokens), half_type),
            pltpu.VMEM((reach // 2 + 1, HEAD_SIZE, tokens), half_type),
            pltpu.VMEM((2, HEAD_SIZE, tokens), half_type),
            pltpu.VMEM((ctx_count,) + block, half_type),
            pltpu.VMEM((ctx_count // 2,) + block, half_type),
            pltpu.VMEM((ctx_count // 2,) + block, half_type),
            pltpu.SemaphoreType.DMA((64,)),
            pltpu.SemaphoreType.DMA((ctx_count,)),
            pltpu.SemaphoreType.DMA((reach + 1, 2)),
            pltpu.SemaphoreType.DMA((head_count,)),
            pltpu.SemaphoreType.DMA((head_count,)),
            pltpu.SemaphoreType.DMA((reach + 1,)),
            pltpu.SemaphoreType.DMA((reach // 2 + 1,)),
            pltpu.SemaphoreType.DMA((2,)),
            pltpu.SemaphoreType.DMA((ctx_count // 2,)),
            pltpu.SemaphoreType.DMA((ctx_count // 2,)),
        ]
        + [pltpu.VMEM(arg.shape, arg.dtype) for arg in args[:11]]
        + [pltpu.SMEM(arg.shape, arg.dtype) for arg in args[11:]]
        + [pltpu.SemaphoreType.DMA((len(args),))],
        compiler_params=pltpu.CompilerParams(
            collective_id=0, has_side_effects=True, vmem_limit_bytes=VMEM_GRANT
        ),
    )(*args)


def on_any_mesh(*args):
    fits = (
        min(8, lax.axis_size("ctx") // 2) == 4
        and lax.axis_size("ctx") % 2 == 0
        and args[4].shape[0] % 8 == 0
        and lax.axis_size("head") == 2 * KVH
    )
    return tuple(publish(fused(*args))) if fits else on_device(*args)


def solution(mesh):
    placed = (
        P("ctx", "head"),
        P("ctx", None),
        P("ctx", "head"),
        P("ctx", "head"),
        P("ctx", "head"),
        P("ctx", "head"),
        P("ctx", "head"),
        P("ctx", "head"),
        P("ctx", "head"),
        P("ctx", "head"),
        P(),
        P(),
        P(),
    )
    return jax.shard_map(
        on_any_mesh,
        mesh=mesh,
        in_specs=placed,
        out_specs=(
            P("ctx", "head"),
            P("ctx", "head"),
            P("ctx", "head"),
            P("ctx", "head"),
            P("ctx", "head"),
            P("ctx", "head"),
            P("ctx", "head"),
            P("ctx", "head"),
            P("ctx", "head"),
        ),
        check_vma=False,
    )
```
